128 devices in a mesh: grp: 4 (over y), dev: 32 (over z, x, core).
Axes of the slice: x: 4, y: 4, z: 4, core: 2. Of those that a mesh axis runs over, the one named last changes fastest.
Arguments:
- voltages: bfloat16 [2, 1024, 65536], P(None, 'dev', 'grp'), may hold values from -6 to 6
- history: bfloat16 [2, 1024, 12288], P(None, 'dev'), may hold values from -6 to 6
- pfb_taps: float32 [4, 4096], replicated, may hold values from -3 to 3
- chan_map: int32 [4096], replicated, may hold values from 0 to 4095, each once
- flag_lists: int32 [512, 12], replicated, may hold values from 0 to 4095, as said below
- beam_index: int32 [256, 1024], replicated, may hold values from 0 to 63
- beam_table: float32 [2, 64], replicated, may hold values from -4 to 4
Outputs:
- visibilities: bfloat16 [128, 2, 2, 1024, 1024], P(('grp', 'dev'))
- beam_power: float32 [2, 256, 4096], P(None, None, ('grp', 'dev'))
The draws below stay inside these ranges and needn't reach their ends.
Inputs may be any that keep to these rules, and one draw needn't show every extreme that they name: `flag_lists`: channel numbers; a list may name a channel twice.
All inputs are finite; a program needn't handle non-finite values.
Results may differ from the reference program's by a relative error of at most 0.0054.
Values may be sent and summed in bfloat16 or wider, within the bound.
A program may use at most 128 MiB of HBM per device.

```python
import math
import jax
import jax.numpy as jnp
from jax import lax

STATIONS = 512
C = 4096
NBEAM = 256
TAPS = 4
SPECTRA_PER_INT = 8
INTEG = 2
NTAB = 64
FLAGS = 12
INPUTS = 1024
SPEC = 16
IN_DEV = 32
NBIN = 128
CH_DEV = 32
N_DEV = 32


def draw_flag_lists(key, part):
    key = jax.random.fold_in(key, 7)
    key_shared, key_station, key_choose = jax.random.split(key, 3)
    shared = jax.random.randint(key_shared, (FLAGS,), 0, C)
    station_own = jax.random.randint(key_station, (STATIONS, FLAGS), 0, C)
    choose_shared = jax.random.randint(key_choose, (STATIONS, FLAGS), 0, 2)
    lists = jnp.where(choose_shared == 1, shared[None, :], station_own).astype(jnp.int32)
    lists = lists.at[0, 0].set(0)
    lists = lists.at[0, 1].set(C - 1)
    return lists.astype(jnp.int32)


def place_ends(entries, own_key, low, top_value):
    longest = entries.shape.index(max(entries.shape))
    spots = []
    for shift in (0, 1):
        where = [jax.random.randint(jax.random.fold_in(own_key, axis), (), 0, length) for axis, length in enumerate(entries.shape)]
        where[longest] = (where[longest] + shift) % entries.shape[longest]
        spots.append(tuple(where))
    return entries.at[spots[0]].set(low).at[spots[1]].set(top_value)


def steps_of(own_key, dims, shards, smallest, largest):
    gain = 1.0
    for position, parts in shards:
        steps = jax.random.uniform(jax.random.fold_in(jax.random.fold_in(own_key, 6), position), (parts,), jnp.float32, smallest / len(shards), largest / len(shards))
        gain = gain * jnp.repeat(jnp.exp(steps), dims[position] // parts).reshape((-1,) + (1,) * (len(dims) - 1 - position))
    return gain


def bell_draw(own_key, extent, deviation, most, cuts=(), held_as=jnp.bfloat16):
    drawn = jax.random.normal(own_key, extent, jnp.float32) * deviation
    if len(cuts) > 0:
        drawn = steps_of(own_key, extent, cuts, -0.22, 0.18) * drawn
    return jnp.clip(drawn, min=-most, max=most).astype(held_as)


def setup_inputs(seed: int = 0) -> dict:
    keys = jax.random.split(jax.random.key(seed), 8)
    return {
        "voltages": bell_draw(keys[0], (2, INPUTS, SPEC * C), 1.0, 6.0, ((1, 32), (2, 4))),
        "history": bell_draw(keys[1], (2, INPUTS, (TAPS - 1) * C), 1.0, 6.0, ((1, 32),)),
        "pfb_taps": bell_draw(keys[2], (TAPS, C), 0.5, 3.0, (), jnp.float32),
        "chan_map": jax.random.permutation(keys[3], C).astype(jnp.int32),
        "flag_lists": draw_flag_lists(jax.random.fold_in(keys[7], 71), 0),
        "beam_index": place_ends(jax.random.randint(keys[5], (NBEAM, INPUTS), 0, NTAB), jax.random.fold_in(keys[5], 1), 0, NTAB - 1).astype(jnp.int32),
        "beam_table": bell_draw(keys[6], (2, NTAB), 1.0, 4.0, (), jnp.float32),
    }


def channelize(group_rows, taps_table):
    blocks = group_rows.reshape(2, group_rows.shape[1], TAPS - 1 + SPEC, C)
    filtered = jnp.zeros((2, group_rows.shape[1], SPEC, C), jnp.float32)
    for tap_number in range(TAPS):
        filtered = filtered + taps_table[tap_number] * blocks[:, :, tap_number:tap_number + SPEC]
    spectra = jnp.fft.fft(filtered[0] + 1j * filtered[1], axis=-1) / math.sqrt(C)
    return jnp.stack([jnp.real(spectra), jnp.imag(spectra)]).astype(jnp.bfloat16)

def reference(voltages, history, pfb_taps, chan_map, flag_lists, beam_index, beam_table):
    series = jnp.concatenate([history, voltages], axis=2)
    grouped = series.reshape(2, N_DEV, IN_DEV, series.shape[2]).transpose(1, 0, 2, 3)
    channel_list = lax.map(lambda group_rows: channelize(group_rows.astype(jnp.float32), pfb_taps), grouped)
    channel_list = channel_list.transpose(1, 0, 2, 3, 4).reshape(2, INPUTS, SPEC, C)
    weight_real = (beam_table[0][beam_index] / math.sqrt(INPUTS)).astype(jnp.bfloat16)
    weight_imag = (beam_table[1][beam_index] / math.sqrt(INPUTS)).astype(jnp.bfloat16)
    real_rows = jnp.concatenate([weight_real, -weight_imag], axis=1)
    imag_rows = jnp.concatenate([weight_imag, weight_real], axis=1)

    def one_bin(bin_number):
        selected_inputs = lax.dynamic_slice_in_dim(chan_map, (bin_number * CH_DEV).astype(jnp.int32), CH_DEV)
        flag_marked = jnp.any(flag_lists[:, :, None] == selected_inputs[None, None, :], axis=1)
        clean_inputs = jnp.repeat(jnp.where(flag_marked, 0.0, 1.0).astype(jnp.float32), 2, axis=0)
        valid_count = SPECTRA_PER_INT * jnp.dot(clean_inputs, clean_inputs.T, precision=lax.Precision.HIGHEST)
        mask_applied = jnp.take(channel_list, selected_inputs, axis=3) * clean_inputs.astype(jnp.bfloat16)[None, :, None, :]
        results = []
        for integration in range(INTEG):
            block = mask_applied[:, :, integration * SPECTRA_PER_INT:(integration + 1) * SPECTRA_PER_INT].reshape(2, INPUTS, SPECTRA_PER_INT * CH_DEV)
            left_rows = jnp.concatenate([block[0], block[1]], axis=1)
            right_rows = jnp.concatenate([block[1], -block[0]], axis=1)
            real_part = jnp.dot(left_rows, left_rows.T, preferred_element_type=jnp.float32)
            imag_part = jnp.dot(right_rows, left_rows.T, preferred_element_type=jnp.float32)
            results.append(jnp.stack([real_part / valid_count, imag_part / valid_count]).astype(jnp.bfloat16))
        columns = mask_applied.reshape(2, INPUTS, SPEC * CH_DEV)
        stacked = jnp.concatenate([columns[0], columns[1]], axis=0)
        beam_real = jnp.dot(real_rows, stacked, preferred_element_type=jnp.float32)
        beam_imag = jnp.dot(imag_rows, stacked, preferred_element_type=jnp.float32)
        powers = (beam_real * beam_real + beam_imag * beam_imag).reshape(NBEAM, INTEG, SPECTRA_PER_INT, CH_DEV)
        return (jnp.stack(results), lax.optimization_barrier(jnp.mean(powers, axis=2)).transpose(1, 0, 2))
    visibilities, powers = lax.map(one_bin, jnp.arange(NBIN, dtype=jnp.int32))
    beam_power = powers.transpose(1, 2, 0, 3).reshape(INTEG, NBEAM, C)
    return (visibilities, beam_power)
```

```python
import math

import numpy as np

import jax
import jax.numpy as jnp
from jax import lax
from jax.experimental import pallas as pl
from jax.experimental.pallas import tpu as pltpu
from jax.sharding import PartitionSpec as P

N1 = 32
N2 = 128
BLK = N1 * N2
ROWS = 32
VMEM_LIMIT = 48 * 1024 * 1024
NT = (((1,), (1,)), ((), ()))


def tables():
    k1 = np.arange(N1)[:, None]
    n2 = np.arange(N2)[None, :]
    turn = 2.0 * np.pi * ((k1 * n2) % BLK) / BLK
    twist = np.stack([np.cos(turn), np.sin(turn)]).astype(np.float32)
    angle = 2.0 * np.pi * ((np.arange(N2)[:, None] * n2) % N2) / N2
    both = np.concatenate([np.cos(angle), np.sin(angle)], axis=1) / math.sqrt(BLK)
    high = both.astype(jnp.bfloat16)
    low = (both - high.astype(np.float64)).astype(jnp.bfloat16)
    return jnp.asarray(twist), jnp.asarray(np.stack([high, low]))


def add(a, b):
    return (a[0] + b[0], a[1] + b[1])


def sub(a, b):
    return (a[0] - b[0], a[1] - b[1])


def minus_i(a):
    return (a[1], -a[0])


def times(a, c, s):
    return (a[0] * c + a[1] * s, a[1] * c - a[0] * s)


def dft4(x):
    a, b = add(x[0], x[2]), sub(x[0], x[2])
    c, d = add(x[1], x[3]), minus_i(sub(x[1], x[3]))
    return [add(a, c), add(b, d), sub(a, c), sub(b, d)]


def dft8(x):
    even = dft4([x[0], x[2], x[4], x[6]])
    odd = dft4([x[1], x[3], x[5], x[7]])
    h = math.sqrt(0.5)
    o1, o3 = odd[1], odd[3]
    odd = [
        odd[0],
        ((o1[0] + o1[1]) * h, (o1[1] - o1[0]) * h),
        minus_i(odd[2]),
        ((o3[1] - o3[0]) * h, (-o3[0] - o3[1]) * h),
    ]
    return [add(even[k], odd[k]) for k in range(4)] + [sub(even[k], odd[k]) for k in range(4)]


def first_stage(src, lane0, row0, taps_ref, twist_ref, mid, high, low, out_row):
    rows = pl.ds(row0, 16)
    for j in range(4):
        points = []
        for a in range(8):
            n1 = 4 * a + j
            total = [None, None]
            for p in range(4):
                tap = taps_ref[pl.ds(p, 1), pl.ds(n1 * N2, N2)]
                for part in range(2):
                    at = pl.multiple_of(lane0 + p * BLK + n1 * N2, N2)
                    term = tap * src[part, rows, pl.ds(at, N2)].astype(jnp.float32)
                    total[part] = term if p == 0 else total[part] + term
            points.append(tuple(total))
        for k, value in enumerate(dft8(points)):
            if j and k:
                turn = 2.0 * math.pi * j * k / N1
                value = times(value, math.cos(turn), math.sin(turn))
            mid[0, k, j] = value[0]
            mid[1, k, j] = value[1]
    for k in range(8):
        column = dft4([(mid[0, k, j], mid[1, k, j]) for j in range(4)])
        for l, value in enumerate(column):
            k1 = k + 8 * l
            if k1:
                value = times(value, twist_ref[0, pl.ds(k1, 1), :], twist_ref[1, pl.ds(k1, 1), :])
            for dst, (re, im) in zip((high, low), split(value)):
                dst[k1, pl.ds(out_row, 16), pl.ds(0, N2)] = re
                dst[k1, pl.ds(out_row, 16), pl.ds(N2, N2)] = im
                dst[k1, pl.ds(64 + out_row, 16), pl.ds(0, N2)] = im
                dst[k1, pl.ds(64 + out_row, 16), pl.ds(N2, N2)] = -re


def split(value):
    high = tuple(v.astype(jnp.bfloat16) for v in value)
    low = tuple((v - h.astype(jnp.float32)).astype(jnp.bfloat16) for v, h in zip(value, high))
    return high, low


def second_stage(k1, dft_ref, high, low, lines):
    part = lax.dot_general(dft_ref[0], high[k1], NT, preferred_element_type=jnp.float32)
    part += lax.dot_general(dft_ref[1], high[k1], NT, preferred_element_type=jnp.float32)
    part += lax.dot_general(dft_ref[0], low[k1], NT, preferred_element_type=jnp.float32)
    lines[pl.ds(pl.multiple_of(k1 * N2, N2), N2), :] = part


def block_turn(picked):
    turned = picked.T
    lane = lax.broadcasted_iota(jnp.int32, (32, 128), 1)
    low5 = (lane & 32) == 0
    low6 = (lane & 64) == 0
    c = [turned[32 * n : 32 * n + 32] for n in range(4)]

    def swap(x, y, low_lanes, step):
        return (
            jnp.where(low_lanes, x, pltpu.roll(y, step, 1)),
            jnp.where(low_lanes, pltpu.roll(x, 128 - step, 1), y),
        )

    c[0], c[1] = swap(c[0], c[1], low5, 32)
    c[2], c[3] = swap(c[2], c[3], low5, 32)
    c[0], c[2] = swap(c[0], c[2], low6, 64)
    c[1], c[3] = swap(c[1], c[3], low6, 64)
    return c


def spectra_kernel(
    windows, line_ref, own, history, halo, taps_ref, twist_ref, dft_ref, out, src, mid, high, low, lines, picked, sem
):
    grp = lax.axis_index("grp")
    n_grp = lax.axis_size("grp")
    copies = []

    def copy_in(source, start, count, at):
        return pltpu.make_async_copy(
            source.at[:, :, pl.ds(start * BLK, count * BLK)], src.at[:, :, pl.ds(at * BLK, count * BLK)], sem
        )

    def move(*parts):
        for source, start, count, at in parts:
            copy = copy_in(source, start, count, at)
            copy.start()
            copy.wait()

    if windows == (0, 4):
        move((own, 0, 4, 0), (halo, 0, 1, 7))

        @pl.when(grp < n_grp - 1)
        def _():
            move((own, 1, 3, 4))

        @pl.when(grp == n_grp - 1)
        def _():
            move((history, 0, 3, 4))

    else:
        move((own, 0, 3, 2))

        @pl.when(grp > 0)
        def _():
            move((halo, 0, 2, 0))

        @pl.when(grp == 0)
        def _():
            move((history, 1, 2, 0))

    for number, window in enumerate(windows):

        @pl.loop(0, ROWS // 16)
        def _(half):
            row0 = pl.multiple_of(half * 16, 16)
            first_stage(src, window * BLK, row0, taps_ref, twist_ref, mid, high, low, number * 32 + row0)

    @pl.loop(0, N1)
    def _(k1):
        second_stage(k1, dft_ref, high, low, lines)

    @pl.loop(0, 32)
    def _(group):
        for n in range(128):
            picked[pl.ds(n, 1), :] = lines[pl.ds(line_ref[group * 128 + n], 1), :]
        for n, block in enumerate(block_turn(picked[...])):
            out[group * 4 + n] = block.astype(jnp.bfloat16)


def spectra(windows, line, own, history, halo, taps, twist, dft):
    whole = pl.BlockSpec(memory_space=pltpu.VMEM)
    anywhere = pl.BlockSpec(memory_space=pl.ANY)
    return pl.pallas_call(
        lambda *refs: spectra_kernel(windows, *refs),
        out_shape=jax.ShapeDtypeStruct((128, 32, 128), jnp.bfloat16),
        in_specs=[pl.BlockSpec(memory_space=pltpu.SMEM), anywhere, anywhere, anywhere, whole, whole, whole],
        out_specs=whole,
        scratch_shapes=[
            pltpu.VMEM((2, ROWS, 8 * BLK), jnp.bfloat16),
            pltpu.VMEM((2, 8, 4, 16, 128), jnp.float32),
            pltpu.VMEM((N1, 128, 256), jnp.bfloat16),
            pltpu.VMEM((N1, 128, 256), jnp.bfloat16),
            pltpu.VMEM((BLK, 128), jnp.float32),
            pltpu.VMEM((128, 128), jnp.float32),
            pltpu.SemaphoreType.DMA,
        ],
        compiler_params=pltpu.CompilerParams(vmem_limit_bytes=VMEM_LIMIT),
        cost_estimate=pl.CostEstimate(flops=10**10, bytes_accessed=5 * 10**6, transcendentals=0),
        name="spectra",
    )(line, own, history, halo, taps, twist, dft)


def side_kernel(flags_ref, mine_ref, index_ref, table_ref, mask_ref, weight_ref, inverse_ref):
    mine = mine_ref[...]
    flagged = flags_ref[:, 0:1] == mine
    for n in range(1, flags_ref.shape[1]):
        flagged = flagged | (flags_ref[:, n : n + 1] == mine)
    mask = jnp.where(flagged, 0.0, 1.0).astype(jnp.bfloat16)
    mask_ref[...] = mask
    for n in range(4):
        rows = pl.ds(n * 256, 256)
        counts = 2.0 * lax.dot_general(mask_ref[rows, :], mask_ref[...], NT, preferred_element_type=jnp.float32)
        inverse_ref[rows, :] = 1.0 / counts
    scale = 1.0 / math.sqrt(index_ref.shape[1])
    table_re = jnp.broadcast_to(table_ref[0:1, :] * scale, (8, 128))
    table_im = jnp.broadcast_to(table_ref[1:2, :] * scale, (8, 128))

    @pl.loop(0, index_ref.shape[0] // 16)
    def _(step):
        at = pl.multiple_of(step * 16, 16)
        for n in range(index_ref.shape[1] // 128):
            cols = pl.ds(n * 128, 128)
            re, im = [], []
            for half in range(2):
                index = index_ref[pl.ds(at + 8 * half, 8), cols]
                re.append(jnp.take_along_axis(table_re, index, axis=1, mode="promise_in_bounds"))
                im.append(jnp.take_along_axis(table_im, index, axis=1, mode="promise_in_bounds"))
            weight_ref[pl.ds(at, 16), cols] = jnp.concatenate(re, axis=0).astype(jnp.bfloat16)
            weight_ref[pl.ds(256 + at, 16), cols] = jnp.concatenate(im, axis=0).astype(jnp.bfloat16)


def side(flags, mine, index, table):
    whole = pl.BlockSpec(memory_space=pltpu.VMEM)
    return pl.pallas_call(
        side_kernel,
        out_shape=(
            jax.ShapeDtypeStruct((1024, 128), jnp.bfloat16),
            jax.ShapeDtypeStruct((512, 1024), jnp.bfloat16),
            jax.ShapeDtypeStruct((1024, 1024), jnp.float32),
        ),
        in_specs=[whole] * 4,
        out_specs=(whole,) * 3,
        compiler_params=pltpu.CompilerParams(vmem_limit_bytes=VMEM_LIMIT),
        cost_estimate=pl.CostEstimate(flops=3 * 10**9, bytes_accessed=6 * 10**6, transcendentals=0),
        name="side",
    )(flags, mine, index, table)


def correlate_kernel(later, earlier, mask_ref, weight_ref, inverse_ref, vis_ref, power_ref, left, right):
    step = pl.program_id(0)
    lane = lax.broadcasted_iota(jnp.int32, (256, 128), 1)
    real_lane = lane < 64

    @pl.when(step == 0)
    def _():
        @pl.loop(0, 4)
        def _(n):
            rows = pl.ds(pl.multiple_of(n * 256, 256), 256)
            mask = mask_ref[rows, :].astype(jnp.float32)
            first = (lane & 32) == 0
            one = later[1, rows, :].astype(jnp.float32)
            three = later[3, rows, :].astype(jnp.float32)
            blocks = (
                (later[0, rows, :], earlier[0, rows, :], earlier[1, rows, :], jnp.where(first, one, three)),
                (later[2, rows, :], earlier[2, rows, :], earlier[3, rows, :], jnp.where(first, three, one)),
            )
            for t in range(2):
                for b in range(4):
                    masked = blocks[t][b].astype(jnp.float32) * mask
                    crossed = pltpu.roll(masked, 64, 1)
                    left[t, rows, pl.ds(b * 128, 128)] = masked.astype(jnp.bfloat16)
                    right[t, rows, pl.ds(b * 128, 128)] = jnp.where(real_lane, crossed, -crossed).astype(jnp.bfloat16)

        for t in range(2):
            total = jnp.zeros((256, 128), jnp.float32)
            product = jnp.dot(weight_ref[...], left[t], preferred_element_type=jnp.float32)
            for b in range(4):
                by_real = product[:256, b * 128 : b * 128 + 128]
                by_imag = pltpu.roll(product[256:, b * 128 : b * 128 + 128], 64, 1)
                beam = by_real + jnp.where(real_lane, -by_imag, by_imag)
                total += beam * beam
            total += pltpu.roll(total, 64, 1)
            total += pltpu.roll(total, 32, 1)
            power_ref[t] = total[:, :32] * 0.125

    rows = pl.ds(pl.multiple_of(step * 256, 256), 256)
    inverse = inverse_ref[...]
    for t in range(2):
        for part, lhs in enumerate((left, right)):
            value = lax.dot_general(lhs[t, rows, :], left[t], NT, preferred_element_type=jnp.float32)
            vis_ref[0, t, part] = (value * inverse).astype(jnp.bfloat16)


def correlate(later, earlier, mask, weight, inverse):
    return pl.pallas_call(
        correlate_kernel,
        grid=(4,),
        out_shape=(
            jax.ShapeDtypeStruct((1, 2, 2, 1024, 1024), jnp.bfloat16),
            jax.ShapeDtypeStruct((2, 256, 32), jnp.float32),
        ),
        in_specs=[
            pl.BlockSpec((4, 1024, 128), lambda i: (0, 0, 0)),
            pl.BlockSpec((4, 1024, 128), lambda i: (0, 0, 0)),
            pl.BlockSpec((1024, 128), lambda i: (0, 0)),
            pl.BlockSpec((512, 1024), lambda i: (0, 0)),
            pl.BlockSpec((256, 1024), lambda i: (i, 0)),
        ],
        out_specs=(
            pl.BlockSpec((1, 2, 2, 256, 1024), lambda i: (0, 0, 0, i, 0)),
            pl.BlockSpec((2, 256, 32), lambda i: (0, 0, 0)),
        ),
        scratch_shapes=[pltpu.VMEM((2, 1024, 512), jnp.bfloat16)] * 2,
        compiler_params=pltpu.CompilerParams(vmem_limit_bytes=VMEM_LIMIT),
        cost_estimate=pl.CostEstimate(flops=6 * 10**9, bytes_accessed=16 * 10**6, transcendentals=0),
        name="correlate",
    )(later, earlier, mask, weight, inverse)


def per_device(voltages, history, pfb_taps, chan_map, flag_lists, beam_index, beam_table):
    n_grp = lax.axis_size("grp")
    n_dev = lax.axis_size("dev")
    twist, dft = tables()
    after = lax.ppermute(voltages[:, :, :BLK], "grp", [(n, (n - 1) % n_grp) for n in range(n_grp)])
    before = lax.ppermute(voltages[:, :, 2 * BLK :], "grp", [(n, n + 1) for n in range(n_grp - 1)])
    line = (chan_map % N1) * N2 + chan_map // N1
    later = spectra((0, 4), line, voltages, history, after, pfb_taps, twist, dft)
    later = lax.all_to_all(later, ("grp", "dev"), split_axis=0, concat_axis=0, tiled=True)
    earlier = spectra((0, 1), line, voltages, history, before, pfb_taps, twist, dft)
    earlier = lax.all_to_all(earlier, ("grp", "dev"), split_axis=0, concat_axis=0, tiled=True)

    my_bin = lax.axis_index("grp") * n_dev + lax.axis_index("dev")
    mine = jnp.tile(lax.dynamic_slice_in_dim(chan_map, my_bin * 32, 32), 4)[None, :]
    table = jnp.pad(beam_table, ((0, 0), (0, 64)))
    mask, weight, inverse = side(jnp.repeat(flag_lists, 2, axis=0), mine, beam_index, table)
    return correlate(later.reshape(4, 1024, 128), earlier.reshape(4, 1024, 128), mask, weight, inverse)


def solution(mesh):
    placed = (P(None, "dev", "grp"), P(None, "dev", None), P(), P(), P(), P(), P())
    return jax.shard_map(
        per_device,
        mesh=mesh,
        in_specs=placed,
        out_specs=(P(("grp", "dev"), None, None, None, None), P(None, None, ("grp", "dev"))),
        check_vma=False,
    )
```

```python
import math

import numpy as np

import jax
import jax.numpy as jnp
from jax import lax
from jax.experimental import pallas as pl
from jax.experimental.pallas import tpu as pltpu
from jax.sharding import PartitionSpec as P

N1 = 32
N2 = 128
BLK = N1 * N2
ROWS = 32
FIRST_LIMIT = 60 * 1024 * 1024
VMEM_LIMIT = 48 * 1024 * 1024
NT = (((1,), (1,)), ((), ()))


def tables():
    k1 = np.arange(N1)[:, None]
    n2 = np.arange(N2)[None, :]
    turn = 2.0 * np.pi * ((k1 * n2) % BLK) / BLK
    twist = np.stack([np.cos(turn), np.sin(turn)]).astype(np.float32)
    angle = 2.0 * np.pi * ((np.arange(N2)[:, None] * n2) % N2) / N2
    both = np.concatenate([np.cos(angle), np.sin(angle)], axis=1) / math.sqrt(BLK)
    high = both.astype(jnp.bfloat16)
    low = (both - high.astype(np.float64)).astype(jnp.bfloat16)
    return jnp.asarray(twist), jnp.asarray(np.stack([high, low]))


def add(a, b):
    return (a[0] + b[0], a[1] + b[1])


def sub(a, b):
    return (a[0] - b[0], a[1] - b[1])


def minus_i(a):
    return (a[1], -a[0])


def times(a, c, s):
    return (a[0] * c + a[1] * s, a[1] * c - a[0] * s)


def dft4(x):
    a, b = add(x[0], x[2]), sub(x[0], x[2])
    c, d = add(x[1], x[3]), minus_i(sub(x[1], x[3]))
    return [add(a, c), add(b, d), sub(a, c), sub(b, d)]


def dft8(x):
    even = dft4([x[0], x[2], x[4], x[6]])
    odd = dft4([x[1], x[3], x[5], x[7]])
    h = math.sqrt(0.5)
    o1, o3 = odd[1], odd[3]
    odd = [
        odd[0],
        ((o1[0] + o1[1]) * h, (o1[1] - o1[0]) * h),
        minus_i(odd[2]),
        ((o3[1] - o3[0]) * h, (-o3[0] - o3[1]) * h),
    ]
    return [add(even[k], odd[k]) for k in range(4)] + [sub(even[k], odd[k]) for k in range(4)]


def first_stage(src, lane0, row0, taps_ref, twist_ref, mid, high, low, out_row):
    rows = pl.ds(row0, 16)
    for j in range(4):
        points = []
        for a in range(8):
            n1 = 4 * a + j
            total = [None, None]
            for p in range(4):
                tap = taps_ref[pl.ds(p, 1), pl.ds(n1 * N2, N2)]
                for part in range(2):
                    at = pl.multiple_of(lane0 + p * BLK + n1 * N2, N2)
                    term = tap * src[part, rows, pl.ds(at, N2)].astype(jnp.float32)
                    total[part] = term if p == 0 else total[part] + term
            points.append(tuple(total))
        for k, value in enumerate(dft8(points)):
            if j and k:
                turn = 2.0 * math.pi * j * k / N1
                value = times(value, math.cos(turn), math.sin(turn))
            mid[0, k, j] = value[0]
            mid[1, k, j] = value[1]
    for k in range(8):
        column = dft4([(mid[0, k, j], mid[1, k, j]) for j in range(4)])
        for l, value in enumerate(column):
            k1 = k + 8 * l
            if k1:
                value = times(value, twist_ref[0, pl.ds(k1, 1), :], twist_ref[1, pl.ds(k1, 1), :])
            for dst, (re, im) in zip((high, low), split(value)):
                dst[k1, pl.ds(out_row, 16), pl.ds(0, N2)] = re
                dst[k1, pl.ds(out_row, 16), pl.ds(N2, N2)] = im
                dst[k1, pl.ds(64 + out_row, 16), pl.ds(0, N2)] = im
                dst[k1, pl.ds(64 + out_row, 16), pl.ds(N2, N2)] = -re


def split(value):
    high = tuple(v.astype(jnp.bfloat16) for v in value)
    low = tuple((v - h.astype(jnp.float32)).astype(jnp.bfloat16) for v, h in zip(value, high))
    return high, low


def second_stage(k1, dft_ref, high, low, lines):
    part = lax.dot_general(dft_ref[0], high[k1], NT, preferred_element_type=jnp.float32)
    part += lax.dot_general(dft_ref[1], high[k1], NT, preferred_element_type=jnp.float32)
    part += lax.dot_general(dft_ref[0], low[k1], NT, preferred_element_type=jnp.float32)
    lines[pl.ds(k1, N2, stride=N1), :] = part


def block_turn(picked):
    turned = picked.astype(jnp.bfloat16).T
    lane = lax.broadcasted_iota(jnp.int32, (32, 128), 1)
    low5 = (lane & 32) == 0
    low6 = (lane & 64) == 0
    c = [turned[32 * n : 32 * n + 32] for n in range(4)]

    def swap(x, y, low_lanes, step):
        return (
            jnp.where(low_lanes, x, pltpu.roll(y, step, 1)),
            jnp.where(low_lanes, pltpu.roll(x, 128 - step, 1), y),
        )

    c[0], c[1] = swap(c[0], c[1], low5, 32)
    c[2], c[3] = swap(c[2], c[3], low5, 32)
    c[0], c[2] = swap(c[0], c[2], low6, 64)
    c[1], c[3] = swap(c[1], c[3], low6, 64)
    return c


def side_work(my_bin, chan_ref, flags_ref, index_ref, table_ref, mask_ref, weight_ref, inverse_ref, twice):
    lane = lax.broadcasted_iota(jnp.int32, (8, 128), 1) & 31
    mine = jnp.zeros((8, 128), jnp.int32)
    for q in range(32):
        mine = jnp.where(lane == q, chan_ref[my_bin * 32 + q], mine)
    mine = mine[0:1]
    flagged = flags_ref[:, 0:1] == mine
    for n in range(1, flags_ref.shape[1]):
        flagged = flagged | (flags_ref[:, n : n + 1] == mine)
    clean = jnp.where(flagged, 0.0, 1.0)
    twice[pl.ds(0, 512, stride=2), :] = clean
    twice[pl.ds(1, 512, stride=2), :] = clean
    mask_ref[...] = twice[...].astype(jnp.bfloat16)

    @pl.loop(0, 8)
    def _(n):
        rows = pl.ds(pl.multiple_of(n * 128, 128), 128)
        counts = 2.0 * lax.dot_general(mask_ref[rows, :], mask_ref[...], NT, preferred_element_type=jnp.float32)
        inverse_ref[rows, :] = 1.0 / counts

    scale = 1.0 / math.sqrt(index_ref.shape[1])
    table = jnp.concatenate([table_ref[...], table_ref[...]], axis=1) * scale
    table_re = jnp.broadcast_to(table[0:1, :], (8, 128))
    table_im = jnp.broadcast_to(table[1:2, :], (8, 128))

    @pl.loop(0, index_ref.shape[0] // 16)
    def _(step):
        at = pl.multiple_of(step * 16, 16)
        for n in range(index_ref.shape[1] // 128):
            cols = pl.ds(n * 128, 128)
            re, im = [], []
            for half in range(2):
                index = index_ref[pl.ds(at + 8 * half, 8), cols]
                re.append(jnp.take_along_axis(table_re, index, axis=1, mode="promise_in_bounds"))
                im.append(jnp.take_along_axis(table_im, index, axis=1, mode="promise_in_bounds"))
            weight_ref[pl.ds(at, 16), cols] = jnp.concatenate(re, axis=0).astype(jnp.bfloat16)
            weight_ref[pl.ds(256 + at, 16), cols] = jnp.concatenate(im, axis=0).astype(jnp.bfloat16)


def spectra_kernel(
    chan_ref, own, history, taps_hbm, twist_hbm, dft_hbm, flags_hbm, index_hbm, table_ref,
    arrived, mask_ref, weight_ref, inverse_ref,
    src, mid, high, low, lines, picked, out, taps_ref, twist_ref, dft_ref, flags_ref, index_ref, twice,
    load_sem, own_sem, rim_sem, halo_send, halo_recv, send_sem, recv_sem,
):
    grp, dev = lax.axis_index("grp"), lax.axis_index("dev")
    n_grp, n_dev = lax.axis_size("grp"), lax.axis_size("dev")
    count = n_grp * n_dev
    me = grp * n_dev + dev
    left, right = lax.rem(grp + n_grp - 1, n_grp), lax.rem(grp + 1, n_grp)
    is_first, is_last = grp == 0, grp == n_grp - 1
    barrier = pltpu.get_barrier_semaphore()

    @pl.loop(1, count)
    def _(n):
        peer = lax.rem(me + n, count)
        pl.semaphore_signal(
            barrier, inc=1, device_id=(peer // n_dev, lax.rem(peer, n_dev)), device_id_type=pl.DeviceIdType.MESH
        )

    def blocks(ref, start, number):
        return ref.at[:, :, pl.ds(pl.multiple_of(start * BLK, BLK), number * BLK)]

    loads = [
        pltpu.make_async_copy(taps_hbm, taps_ref, load_sem.at[0]),
        pltpu.make_async_copy(twist_hbm, twist_ref, load_sem.at[1]),
        pltpu.make_async_copy(dft_hbm, dft_ref, load_sem.at[2]),
        pltpu.make_async_copy(flags_hbm, flags_ref, load_sem.at[3]),
        pltpu.make_async_copy(index_hbm, index_ref, load_sem.at[4]),
        pltpu.make_async_copy(own, blocks(src, 2, 4), own_sem),
    ]
    for load in reversed(loads):
        load.start()
    rim_first = pltpu.make_async_copy(blocks(history, 1, 2), blocks(src, 0, 2), rim_sem)
    rim_last = pltpu.make_async_copy(blocks(history, 0, 3), blocks(src, 7, 3), rim_sem)

    @pl.when(is_first)
    def _():
        rim_first.start()

    @pl.when(is_last)
    def _():
        rim_last.start()

    def halo(block, at, slot, target):
        return pltpu.make_async_remote_copy(
            src_ref=blocks(own, block, 1),
            dst_ref=blocks(src, at, 1),
            send_sem=halo_send.at[slot],
            recv_sem=halo_recv.at[slot],
            device_id=(target, dev),
            device_id_type=pl.DeviceIdType.MESH,
        )

    after = halo(0, jnp.where(is_first, 10, 6), 0, left)
    near = halo(3, 1, 1, right)
    far = halo(2, 0, 2, right)

    pl.semaphore_wait(barrier, count - 1)
    after.start()

    @pl.when(jnp.logical_not(is_last))
    def _():
        near.start()
        far.start()

    for load in loads:
        load.wait()

    def filtered(window, line):
        @pl.loop(0, ROWS // 16)
        def _(half):
            row0 = pl.multiple_of(half * 16, 16)
            first_stage(src, window * BLK, row0, taps_ref, twist_ref, mid, high, low, line + row0)

    def finish(batch):
        @pl.loop(0, N1 // 4)
        def _(step):
            for n in range(4):
                second_stage(step * 4 + n, dft_ref, high, low, lines)

        @pl.loop(0, 8)
        def _(step):
            at = lax.rem(step + me // 16, 8) * 16
            for part in range(4):
                for n in range(128):
                    row = chan_ref[(at + part * 4) * 32 + n]
                    picked[part, pl.ds(n, 1), :] = lines[pl.ds(row, 1), :]
                for n, block in enumerate(block_turn(picked[part])):
                    out[batch, at + part * 4 + n] = block.astype(jnp.bfloat16)

            @pl.loop(0, 16)
            def _(n):
                peer = at + n

                @pl.when(peer != me)
                def _():
                    pltpu.make_async_remote_copy(
                        src_ref=out.at[batch, peer],
                        dst_ref=arrived.at[batch, me],
                        send_sem=send_sem.at[batch],
                        recv_sem=recv_sem.at[batch],
                        device_id=(peer // n_dev, lax.rem(peer, n_dev)),
                        device_id_type=pl.DeviceIdType.MESH,
                    ).start()

                @pl.when(peer == me)
                def _():
                    pltpu.make_async_copy(out.at[batch, me], arrived.at[batch, me], recv_sem.at[batch]).start()

    filtered(2, 0)
    side_work(me, chan_ref, flags_ref, index_ref, table_ref, mask_ref, weight_ref, inverse_ref, twice)

    @pl.when(is_last)
    def _():
        rim_last.wait()

    after.wait_recv()
    filtered(jnp.where(is_last, 7, 3), 32)
    finish(0)

    @pl.when(is_first)
    def _():
        rim_first.wait()

    @pl.when(jnp.logical_not(is_first))
    def _():
        near.wait_recv()

    filtered(1, 32)

    @pl.when(jnp.logical_not(is_first))
    def _():
        far.wait_recv()

    filtered(0, 0)
    finish(1)

    after.wait_send()

    @pl.when(jnp.logical_not(is_last))
    def _():
        near.wait_send()
        far.wait_send()

    for batch in range(2):
        sent = out.at[batch, pl.ds(0, count - 1)]
        pltpu.make_async_copy(sent, sent, send_sem.at[batch]).wait()
        pltpu.make_async_copy(arrived.at[batch], arrived.at[batch], recv_sem.at[batch]).wait()


def spectra(chan_map, voltages, history, taps, twist, dft, flags, index, table):
    whole = pl.BlockSpec(memory_space=pltpu.VMEM)
    anywhere = pl.BlockSpec(memory_space=pl.ANY)
    return pl.pallas_call(
        spectra_kernel,
        out_shape=(
            jax.ShapeDtypeStruct((2, 128, 32, 128), jnp.bfloat16),
            jax.ShapeDtypeStruct((1024, 128), jnp.bfloat16),
            jax.ShapeDtypeStruct((512, 1024), jnp.bfloat16),
            jax.ShapeDtypeStruct((1024, 1024), jnp.float32),
        ),
        in_specs=[pl.BlockSpec(memory_space=pltpu.SMEM)] + [anywhere] * 7 + [whole],
        out_specs=(anywhere, whole, whole, whole),
        scratch_shapes=[
            pltpu.VMEM((2, ROWS, 11 * BLK), jnp.bfloat16),
            pltpu.VMEM((2, 8, 4, 16, 128), jnp.float32),
            pltpu.VMEM((N1, 128, 256), jnp.bfloat16),
            pltpu.VMEM((N1, 128, 256), jnp.bfloat16),
            pltpu.VMEM((BLK, 128), jnp.float32),
            pltpu.VMEM((4, 128, 128), jnp.float32),
            pltpu.VMEM((2, 128, 32, 128), jnp.bfloat16),
            pltpu.VMEM(taps.shape, taps.dtype),
            pltpu.VMEM(twist.shape, twist.dtype),
            pltpu.VMEM(dft.shape, dft.dtype),
            pltpu.VMEM(flags.shape, flags.dtype),
            pltpu.VMEM(index.shape, index.dtype),
            pltpu.VMEM((1024, 128), jnp.float32),
            pltpu.SemaphoreType.DMA((5,)),
            pltpu.SemaphoreType.DMA,
            pltpu.SemaphoreType.DMA,
            pltpu.SemaphoreType.DMA((3,)),
            pltpu.SemaphoreType.DMA((3,)),
            pltpu.SemaphoreType.DMA((2,)),
            pltpu.SemaphoreType.DMA((2,)),
        ],
        compiler_params=pltpu.CompilerParams(
            vmem_limit_bytes=FIRST_LIMIT, collective_id=0, has_side_effects=True
        ),
        cost_estimate=pl.CostEstimate(flops=10**10, bytes_accessed=10**7, transcendentals=0),
        name="spectra",
    )(chan_map, voltages, history, taps, twist, dft, flags, index, table)


def correlate_kernel(arrived, mask_ref, weight_ref, inverse_ref, vis_ref, power_ref, left, right):
    later, earlier = arrived.at[0], arrived.at[1]
    step = pl.program_id(0)
    lane = lax.broadcasted_iota(jnp.int32, (256, 128), 1)
    real_lane = lane < 64

    @pl.when(step == 0)
    def _():
        @pl.loop(0, 4)
        def _(n):
            rows = pl.ds(pl.multiple_of(n * 256, 256), 256)
            mask = mask_ref[rows, :].astype(jnp.float32)
            first = (lane & 32) == 0
            one = later[1, rows, :].astype(jnp.float32)
            three = later[3, rows, :].astype(jnp.float32)
            blocks = (
                (later[0, rows, :], earlier[0, rows, :], earlier[1, rows, :], jnp.where(first, one, three)),
                (later[2, rows, :], earlier[2, rows, :], earlier[3, rows, :], jnp.where(first, three, one)),
            )
            for t in range(2):
                for b in range(4):
                    masked = blocks[t][b].astype(jnp.float32) * mask
                    crossed = pltpu.roll(masked, 64, 1)
                    left[t, rows, pl.ds(b * 128, 128)] = masked.astype(jnp.bfloat16)
                    right[t, rows, pl.ds(b * 128, 128)] = jnp.where(real_lane, crossed, -crossed).astype(jnp.bfloat16)

        for t in range(2):
            total = jnp.zeros((256, 128), jnp.float32)
            product = jnp.dot(weight_ref[...], left[t], preferred_element_type=jnp.float32)
            for b in range(4):
                by_real = product[:256, b * 128 : b * 128 + 128]
                by_imag = pltpu.roll(product[256:, b * 128 : b * 128 + 128], 64, 1)
                beam = by_real + jnp.where(real_lane, -by_imag, by_imag)
                total += beam * beam
            total += pltpu.roll(total, 64, 1)
            total += pltpu.roll(total, 32, 1)
            power_ref[t] = (total * 0.125).T[:32]

    rows = pl.ds(pl.multiple_of(step * 256, 256), 256)
    inverse = inverse_ref[...]
    for t in range(2):
        for part, lhs in enumerate((left, right)):
            value = lax.dot_general(lhs[t, rows, :], left[t], NT, preferred_element_type=jnp.float32)
            vis_ref[0, t, part] = (value * inverse).astype(jnp.bfloat16)


def correlate(arrived, mask, weight, inverse):
    return pl.pallas_call(
        correlate_kernel,
        grid=(4,),
        out_shape=(
            jax.ShapeDtypeStruct((1, 2, 2, 1024, 1024), jnp.bfloat16),
            jax.ShapeDtypeStruct((2, 32, 256), jnp.float32),
        ),
        in_specs=[
            pl.BlockSpec((2, 4, 1024, 128), lambda i: (0, 0, 0, 0)),
            pl.BlockSpec((1024, 128), lambda i: (0, 0)),
            pl.BlockSpec((512, 1024), lambda i: (0, 0)),
            pl.BlockSpec((256, 1024), lambda i: (i, 0)),
        ],
        out_specs=(
            pl.BlockSpec((1, 2, 2, 256, 1024), lambda i: (0, 0, 0, i, 0)),
            pl.BlockSpec((2, 32, 256), lambda i: (0, 0, 0)),
        ),
        scratch_shapes=[pltpu.VMEM((2, 1024, 512), jnp.bfloat16)] * 2,
        compiler_params=pltpu.CompilerParams(vmem_limit_bytes=VMEM_LIMIT),
        cost_estimate=pl.CostEstimate(flops=6 * 10**9, bytes_accessed=16 * 10**6, transcendentals=0),
        name="correlate",
    )(arrived, mask, weight, inverse)


def per_device(voltages, history, pfb_taps, chan_map, flag_lists, beam_index, beam_table):
    twist, dft = tables()
    arrived, mask, weight, inverse = spectra(
        chan_map, voltages, history, pfb_taps, twist, dft, flag_lists, beam_index, beam_table
    )
    visibilities, power = correlate(arrived.reshape(2, 4, 1024, 128), mask, weight, inverse)
    return visibilities, power.transpose(0, 2, 1)


def solution(mesh):
    placed = (P(None, "dev", "grp"), P(None, "dev", None), P(), P(), P(), P(), P())
    return jax.shard_map(
        per_device,
        mesh=mesh,
        in_specs=placed,
        out_specs=(P(("grp", "dev"), None, None, None, None), P(None, None, ("grp", "dev"))),
        check_vma=False,
    )
```

```python
import math

import numpy as np

import jax
import jax.numpy as jnp
from jax import lax
from jax.experimental import pallas as pl
from jax.experimental.pallas import tpu as pltpu
from jax.sharding import PartitionSpec as P

N1 = 32
N2 = 128
BLK = N1 * N2
ROWS = 32
VMEM_LIMIT = 60 * 1024 * 1024
NT = (((1,), (1,)), ((), ()))


def tables():
    k1 = np.arange(N1)[:, None]
    n2 = np.arange(N2)[None, :]
    turn = 2.0 * np.pi * ((k1 * n2) % BLK) / BLK
    twist = np.stack([np.cos(turn), np.sin(turn)]).astype(np.float32)
    angle = 2.0 * np.pi * ((np.arange(N2)[:, None] * n2) % N2) / N2
    both = np.concatenate([np.cos(angle), np.sin(angle)], axis=1) / math.sqrt(BLK)
    high = both.astype(jnp.bfloat16)
    low = (both - high.astype(np.float64)).astype(jnp.bfloat16)
    return jnp.asarray(twist), jnp.asarray(np.stack([high, low]))


def add(a, b):
    return (a[0] + b[0], a[1] + b[1])


def sub(a, b):
    return (a[0] - b[0], a[1] - b[1])


def minus_i(a):
    return (a[1], -a[0])


def times(a, c, s):
    return (a[0] * c + a[1] * s, a[1] * c - a[0] * s)


def dft4(x):
    a, b = add(x[0], x[2]), sub(x[0], x[2])
    c, d = add(x[1], x[3]), minus_i(sub(x[1], x[3]))
    return [add(a, c), add(b, d), sub(a, c), sub(b, d)]


def dft8(x):
    even = dft4([x[0], x[2], x[4], x[6]])
    odd = dft4([x[1], x[3], x[5], x[7]])
    h = math.sqrt(0.5)
    o1, o3 = odd[1], odd[3]
    odd = [
        odd[0],
        ((o1[0] + o1[1]) * h, (o1[1] - o1[0]) * h),
        minus_i(odd[2]),
        ((o3[1] - o3[0]) * h, (-o3[0] - o3[1]) * h),
    ]
    return [add(even[k], odd[k]) for k in range(4)] + [sub(even[k], odd[k]) for k in range(4)]


def first_stage(src, lane0, row0, taps_ref, twist_ref, mid, high, low, out_row):
    rows = pl.ds(row0, 16)
    for j in range(4):
        points = []
        for a in range(8):
            n1 = 4 * a + j
            total = [None, None]
            for p in range(4):
                tap = taps_ref[pl.ds(p, 1), pl.ds(n1 * N2, N2)]
                for part in range(2):
                    at = pl.multiple_of(lane0 + p * BLK + n1 * N2, N2)
                    term = tap * src[part, rows, pl.ds(at, N2)].astype(jnp.float32)
                    total[part] = term if p == 0 else total[part] + term
            points.append(tuple(total))
        for k, value in enumerate(dft8(points)):
            if j and k:
                turn = 2.0 * math.pi * j * k / N1
                value = times(value, math.cos(turn), math.sin(turn))
            mid[0, k, j] = value[0]
            mid[1, k, j] = value[1]
    for k in range(8):
        column = dft4([(mid[0, k, j], mid[1, k, j]) for j in range(4)])
        for l, value in enumerate(column):
            k1 = k + 8 * l
            if k1:
                value = times(value, twist_ref[0, pl.ds(k1, 1), :], twist_ref[1, pl.ds(k1, 1), :])
            for dst, (re, im) in zip((high, low), split(value)):
                dst[k1, pl.ds(out_row, 16), pl.ds(0, N2)] = re
                dst[k1, pl.ds(out_row, 16), pl.ds(N2, N2)] = im
                dst[k1, pl.ds(64 + out_row, 16), pl.ds(0, N2)] = im
                dst[k1, pl.ds(64 + out_row, 16), pl.ds(N2, N2)] = -re


def split(value):
    high = tuple(v.astype(jnp.bfloat16) for v in value)
    low = tuple((v - h.astype(jnp.float32)).astype(jnp.bfloat16) for v, h in zip(value, high))
    return high, low


def second_stage(k1, dft_ref, high, low, lines):
    part = lax.dot_general(dft_ref[0], high[k1], NT, preferred_element_type=jnp.float32)
    part += lax.dot_general(dft_ref[1], high[k1], NT, preferred_element_type=jnp.float32)
    part += lax.dot_general(dft_ref[0], low[k1], NT, preferred_element_type=jnp.float32)
    lines[pl.ds(k1, N2, stride=N1), :] = part


def block_turn(picked):
    turned = picked.astype(jnp.bfloat16).T
    lane = lax.broadcasted_iota(jnp.int32, (32, 128), 1)
    low5 = (lane & 32) == 0
    low6 = (lane & 64) == 0
    c = [turned[32 * n : 32 * n + 32] for n in range(4)]

    def swap(x, y, low_lanes, step):
        return (
            jnp.where(low_lanes, x, pltpu.roll(y, step, 1)),
            jnp.where(low_lanes, pltpu.roll(x, 128 - step, 1), y),
        )

    c[0], c[1] = swap(c[0], c[1], low5, 32)
    c[2], c[3] = swap(c[2], c[3], low5, 32)
    c[0], c[2] = swap(c[0], c[2], low6, 64)
    c[1], c[3] = swap(c[1], c[3], low6, 64)
    return c


def side_work(my_bin, chan_ref, flags_ref, index_ref, table_ref, mask_ref, weight_ref, inverse_ref, twice):
    lane = lax.broadcasted_iota(jnp.int32, (8, 128), 1) & 31
    mine = jnp.zeros((8, 128), jnp.int32)
    for q in range(32):
        mine = jnp.where(lane == q, chan_ref[my_bin * 32 + q], mine)
    mine = jnp.broadcast_to(mine[0:1], (128, 128)).T
    mine = jnp.concatenate([mine] * (flags_ref.shape[1] // 128), axis=1)
    flagged = flags_ref[0:1, :] == mine
    for n in range(1, flags_ref.shape[0]):
        flagged = flagged | (flags_ref[n : n + 1, :] == mine)
    clean = jnp.where(flagged, 0.0, 1.0).T
    twice[pl.ds(0, 512, stride=2), :] = clean
    twice[pl.ds(1, 512, stride=2), :] = clean
    mask_ref[...] = twice[...].astype(jnp.bfloat16)

    @pl.loop(0, 8)
    def _(n):
        rows = pl.ds(pl.multiple_of(n * 128, 128), 128)
        counts = 2.0 * lax.dot_general(mask_ref[rows, :], mask_ref[...], NT, preferred_element_type=jnp.float32)
        inverse_ref[rows, :] = 1.0 / counts

    scale = 1.0 / math.sqrt(index_ref.shape[1])
    table = jnp.concatenate([table_ref[...], table_ref[...]], axis=1) * scale
    table_re = jnp.broadcast_to(table[0:1, :], (8, 128))
    table_im = jnp.broadcast_to(table[1:2, :], (8, 128))

    @pl.loop(0, index_ref.shape[0] // 16)
    def _(step):
        at = pl.multiple_of(step * 16, 16)
        for n in range(index_ref.shape[1] // 128):
            cols = pl.ds(n * 128, 128)
            re, im = [], []
            for half in range(2):
                index = index_ref[pl.ds(at + 8 * half, 8), cols]
                re.append(jnp.take_along_axis(table_re, index, axis=1, mode="promise_in_bounds"))
                im.append(jnp.take_along_axis(table_im, index, axis=1, mode="promise_in_bounds"))
            weight_ref[pl.ds(at, 16), cols] = jnp.concatenate(re, axis=0).astype(jnp.bfloat16)
            weight_ref[pl.ds(256 + at, 16), cols] = jnp.concatenate(im, axis=0).astype(jnp.bfloat16)


def spectra_kernel(
    chan_ref, own, history, taps_hbm, twist_hbm, dft_hbm, flags_hbm, index_hbm, table_hbm,
    arrived, mask_hbm, weight_hbm, inverse_hbm,
    src, mid, high, low, lines, picked, out, taps_ref, twist_ref, dft_ref, flags_ref, index_ref, table_ref,
    twice, mask_ref, weight_ref, inverse_ref,
    load_sem, side_sem, own_sem, rim_sem, halo_send, halo_recv, send_sem, recv_sem,
):
    grp, dev = lax.axis_index("grp"), lax.axis_index("dev")
    n_grp, n_dev = lax.axis_size("grp"), lax.axis_size("dev")
    count = n_grp * n_dev
    me = grp * n_dev + dev
    planes = [lax.rem(grp + n, n_grp) for n in range(n_grp)]
    left, right = planes[n_grp - 1], planes[1]
    is_first, is_last = grp == 0, grp == n_grp - 1
    barrier = pltpu.get_barrier_semaphore()

    for n in (1, 3, 2, 0):

        @pl.loop(0, n_dev, unroll=8)
        def _(peer):
            def greet():
                pl.semaphore_signal(
                    barrier, inc=1, device_id=(planes[n], peer), device_id_type=pl.DeviceIdType.MESH
                )

            if n:
                greet()
            else:
                pl.when(peer != dev)(greet)

    def blocks(ref, start, number, rows=slice(None)):
        return ref.at[:, rows, pl.ds(pl.multiple_of(start * BLK, BLK), number * BLK)]

    low_rows, high_rows = pl.ds(0, 16), pl.ds(16, 16)
    loads = [
        pltpu.make_async_copy(own, blocks(src, 2, 4), own_sem),
        pltpu.make_async_copy(taps_hbm, taps_ref, load_sem.at[0]),
        pltpu.make_async_copy(twist_hbm, twist_ref, load_sem.at[1]),
        pltpu.make_async_copy(dft_hbm, dft_ref, load_sem.at[2]),
        pltpu.make_async_copy(flags_hbm, flags_ref, load_sem.at[3]),
        pltpu.make_async_copy(index_hbm, index_ref, load_sem.at[4]),
        pltpu.make_async_copy(table_hbm, table_ref, load_sem.at[5]),
    ]
    for load in loads:
        load.start()
    rim_first = pltpu.make_async_copy(blocks(history, 1, 2), blocks(src, 0, 2), rim_sem)
    rim_last = pltpu.make_async_copy(blocks(history, 0, 3), blocks(src, 8, 3), rim_sem)

    @pl.when(is_first)
    def _():
        rim_first.start()

    @pl.when(is_last)
    def _():
        rim_last.start()

    def halo(block, at, rows, slot, target):
        return pltpu.make_async_remote_copy(
            src_ref=blocks(own, block, 1, rows),
            dst_ref=blocks(src, at, 1, rows),
            send_sem=halo_send.at[slot],
            recv_sem=halo_recv.at[slot],
            device_id=(target, dev),
            device_id_type=pl.DeviceIdType.MESH,
        )

    from_right = jnp.where(is_first, 11, 6)
    after = halo(0, from_right, pl.ds(0, 32), 0, left)
    beyond = halo(1, from_right + 1, high_rows, 3, left)
    near = halo(3, 1, pl.ds(0, 32), 1, right)
    far = halo(2, 0, low_rows, 2, right)

    pl.semaphore_wait(barrier, count - 1)
    after.start()

    @pl.when(jnp.logical_not(is_last))
    def _():
        near.start()

    beyond.start()

    @pl.when(jnp.logical_not(is_last))
    def _():
        far.start()

    for load in loads:
        load.wait()

    def filtered(window, line, row0):
        first_stage(src, window * BLK, row0, taps_ref, twist_ref, mid, high, low, line + row0)

    def both_halves(window, line):
        @pl.loop(0, ROWS // 16)
        def _(half):
            filtered(window, line, pl.multiple_of(half * 16, 16))

    def finish(batch):
        @pl.loop(0, N1 // 8)
        def _(step):
            for n in range(8):
                second_stage(step * 8 + n, dft_ref, high, low, lines)

        @pl.loop(0, 8)
        def _(step):
            first = lax.rem(step + dev // 4, 8) * 4
            for part in range(n_grp):
                at = planes[part] * n_dev + first
                for n in range(128):
                    picked[part, pl.ds(n, 1), :] = lines[pl.ds(chan_ref[at * 32 + n], 1), :]
                for n, block in enumerate(block_turn(picked[part])):
                    out[batch, at + n] = block.astype(jnp.bfloat16)
            for part in (2, 1, 3, 0):
                for n in range(4):
                    peer = first + n
                    place = planes[part] * n_dev + peer

                    def send():
                        pltpu.make_async_remote_copy(
                            src_ref=out.at[batch, place],
                            dst_ref=arrived.at[batch, me],
                            send_sem=send_sem.at[batch],
                            recv_sem=recv_sem.at[batch],
                            device_id=(planes[part], peer),
                            device_id_type=pl.DeviceIdType.MESH,
                        ).start()

                    if part:
                        send()
                    else:
                        pl.when(peer != dev)(send)

        pltpu.make_async_copy(out.at[batch, me], arrived.at[batch, me], recv_sem.at[batch]).start()

    both_halves(2, 0)
    side_work(me, chan_ref, flags_ref, index_ref, table_ref, mask_ref, weight_ref, inverse_ref, twice)
    side_copies = [
        pltpu.make_async_copy(held, kept, side_sem.at[n])
        for n, (held, kept) in enumerate(
            ((mask_ref, mask_hbm), (weight_ref, weight_hbm), (inverse_ref, inverse_hbm))
        )
    ]
    for copy in side_copies:
        copy.start()

    @pl.when(is_last)
    def _():
        rim_last.wait()

    after.wait_recv()
    both_halves(jnp.where(is_last, 8, 3), 32)
    finish(0)

    @pl.when(is_first)
    def _():
        rim_first.wait()

    @pl.when(jnp.logical_not(is_first))
    def _():
        near.wait_recv()

    both_halves(1, 32)

    @pl.when(jnp.logical_not(is_first))
    def _():
        far.wait_recv()

    filtered(0, 0, 0)
    beyond.wait_recv()
    filtered(jnp.where(is_last, 9, 4), 0, 16)
    finish(1)

    after.wait_send()
    beyond.wait_send()

    @pl.when(jnp.logical_not(is_last))
    def _():
        near.wait_send()
        far.wait_send()

    for copy in side_copies:
        copy.wait()
    for batch in range(2):
        sent = out.at[batch, pl.ds(0, count - 1)]
        pltpu.make_async_copy(sent, sent, send_sem.at[batch]).wait()
        pltpu.make_async_copy(arrived.at[batch], arrived.at[batch], recv_sem.at[batch]).wait()


def spectra(chan_map, *arrays):
    anywhere = pl.BlockSpec(memory_space=pl.ANY)
    side = (
        jax.ShapeDtypeStruct((1024, 128), jnp.bfloat16),
        jax.ShapeDtypeStruct((512, 1024), jnp.bfloat16),
        jax.ShapeDtypeStruct((1024, 1024), jnp.float32),
    )
    return pl.pallas_call(
        spectra_kernel,
        out_shape=(jax.ShapeDtypeStruct((2, 128, 32, 128), jnp.bfloat16),) + side,
        in_specs=[pl.BlockSpec(memory_space=pltpu.SMEM)] + [anywhere] * len(arrays),
        out_specs=(anywhere,) * 4,
        scratch_shapes=[
            pltpu.VMEM((2, ROWS, 13 * BLK), jnp.bfloat16),
            pltpu.VMEM((2, 8, 4, 16, 128), jnp.float32),
            pltpu.VMEM((N1, 128, 256), jnp.bfloat16),
            pltpu.VMEM((N1, 128, 256), jnp.bfloat16),
            pltpu.VMEM((BLK, 128), jnp.float32),
            pltpu.VMEM((4, 128, 128), jnp.float32),
            pltpu.VMEM((2, 128, 32, 128), jnp.bfloat16),
        ]
        + [pltpu.VMEM(array.shape, array.dtype) for array in arrays[2:]]
        + [pltpu.VMEM((1024, 128), jnp.float32)]
        + [pltpu.VMEM(result.shape, result.dtype) for result in side]
        + [
            pltpu.SemaphoreType.DMA((6,)),
            pltpu.SemaphoreType.DMA((3,)),
            pltpu.SemaphoreType.DMA,
            pltpu.SemaphoreType.DMA,
            pltpu.SemaphoreType.DMA((4,)),
            pltpu.SemaphoreType.DMA((4,)),
            pltpu.SemaphoreType.DMA((2,)),
            pltpu.SemaphoreType.DMA((2,)),
        ],
        compiler_params=pltpu.CompilerParams(
            vmem_limit_bytes=VMEM_LIMIT, collective_id=0, has_side_effects=True
        ),
        cost_estimate=pl.CostEstimate(flops=10**10, bytes_accessed=10**7, transcendentals=0),
        name="spectra",
    )(chan_map, *arrays)


def correlate_kernel(arrived_hbm, mask_hbm, weight_hbm, inverse_ref, vis_ref, power_ref, arrived, mask_ref, weight_ref, left, right, sems):
    step = pl.program_id(0)
    lane = lax.broadcasted_iota(jnp.int32, (256, 128), 1)
    row = lax.broadcasted_iota(jnp.int32, (256, 128), 0)
    real_lane = lane < 64
    first = (lane & 32) == 0
    moved = first & ((row & 16) != 0)
    load_mask = pltpu.make_async_copy(mask_hbm, mask_ref, sems.at[4])
    load_weight = pltpu.make_async_copy(weight_hbm, weight_ref, sems.at[5])

    def load_rows(n):
        rows = pl.ds(n * 256, 256)
        return pltpu.make_async_copy(arrived_hbm.at[:, :, rows], arrived.at[:, :, rows], sems.at[n])

    @pl.when(step == 0)
    def _():
        load_mask.start()
        for n in range(4):
            load_rows(n).start()
        load_weight.start()
        load_mask.wait()
        for n in range(4):
            load_rows(n).wait()
            rows = pl.ds(n * 256, 256)
            mask = mask_ref[rows, :].astype(jnp.float32)
            late = [arrived[0, g, rows, :].astype(jnp.float32) for g in range(4)]
            early = [arrived[1, g, rows, :].astype(jnp.float32) for g in range(4)]
            early = [jnp.where(moved, early[(g + 3) % 4], early[g]) for g in range(4)]
            blocks = (
                (late[0], early[0], early[1], jnp.where(first, late[1], late[3])),
                (late[2], early[2], early[3], jnp.where(first, late[3], late[1])),
            )
            for t in range(2):
                for b in range(4):
                    masked = blocks[t][b] * mask
                    crossed = pltpu.roll(masked, 64, 1)
                    left[t, rows, pl.ds(b * 128, 128)] = masked.astype(jnp.bfloat16)
                    right[t, rows, pl.ds(b * 128, 128)] = jnp.where(real_lane, crossed, -crossed).astype(jnp.bfloat16)

    rows = pl.ds(pl.multiple_of(step * 256, 256), 256)
    inverse = inverse_ref[...]
    for t in range(2):
        for part, lhs in enumerate((left, right)):
            value = lax.dot_general(lhs[t, rows, :], left[t], NT, preferred_element_type=jnp.float32)
            vis_ref[0, t, part] = (value * inverse).astype(jnp.bfloat16)

    @pl.when(step == 1)
    def _():
        load_weight.wait()
        for t in range(2):
            total = jnp.zeros((256, 128), jnp.float32)
            product = jnp.dot(weight_ref[...], left[t], preferred_element_type=jnp.float32)
            for b in range(4):
                by_real = product[:256, b * 128 : b * 128 + 128]
                by_imag = pltpu.roll(product[256:, b * 128 : b * 128 + 128], 64, 1)
                beam = by_real + jnp.where(real_lane, -by_imag, by_imag)
                total += beam * beam
            total += pltpu.roll(total, 64, 1)
            total += pltpu.roll(total, 32, 1)
            power_ref[t] = (total * 0.125).T[:32]


def correlate(arrived, mask, weight, inverse):
    anywhere = pl.BlockSpec(memory_space=pl.ANY)
    return pl.pallas_call(
        correlate_kernel,
        grid=(4,),
        out_shape=(
            jax.ShapeDtypeStruct((1, 2, 2, 1024, 1024), jnp.bfloat16),
            jax.ShapeDtypeStruct((2, 32, 256), jnp.float32),
        ),
        in_specs=[anywhere, anywhere, anywhere, pl.BlockSpec((256, 1024), lambda i: (i, 0))],
        out_specs=(
            pl.BlockSpec((1, 2, 2, 256, 1024), lambda i: (0, 0, 0, i, 0)),
            pl.BlockSpec((2, 32, 256), lambda i: (0, 0, 0)),
        ),
        scratch_shapes=[
            pltpu.VMEM(arrived.shape, jnp.bfloat16),
            pltpu.VMEM(mask.shape, jnp.bfloat16),
            pltpu.VMEM(weight.shape, jnp.bfloat16),
            pltpu.VMEM((2, 1024, 512), jnp.bfloat16),
            pltpu.VMEM((2, 1024, 512), jnp.bfloat16),
            pltpu.SemaphoreType.DMA((6,)),
        ],
        compiler_params=pltpu.CompilerParams(vmem_limit_bytes=VMEM_LIMIT),
        cost_estimate=pl.CostEstimate(flops=6 * 10**9, bytes_accessed=16 * 10**6, transcendentals=0),
        name="correlate",
    )(arrived, mask, weight, inverse)


def per_device(voltages, history, pfb_taps, chan_map, flag_lists, beam_index, beam_table):
    twist, dft = tables()
    arrived, mask, weight, inverse = spectra(
        chan_map, voltages, history, pfb_taps, twist, dft, flag_lists.T, beam_index, beam_table
    )
    visibilities, power = correlate(arrived.reshape(2, 4, 1024, 128), mask, weight, inverse)
    return visibilities, power.transpose(0, 2, 1)


def solution(mesh):
    placed = (P(None, "dev", "grp"), P(None, "dev", None), P(), P(), P(), P(), P())
    return jax.shard_map(
        per_device,
        mesh=mesh,
        in_specs=placed,
        out_specs=(P(("grp", "dev"), None, None, None, None), P(None, None, ("grp", "dev"))),
        check_vma=False,
    )
```

```python
import math

import numpy as np

import jax
import jax.numpy as jnp
from jax import lax
from jax.experimental import pallas as pl
from jax.experimental.pallas import tpu as pltpu
from jax.sharding import PartitionSpec as P

N1 = 32
N2 = 128
BLK = N1 * N2
ROWS = 32
VMEM_LIMIT = 48 * 1024 * 1024
NT = (((1,), (1,)), ((), ()))


def tables():
    k1 = np.arange(N1)[:, None]
    n2 = np.arange(N2)[None, :]
    turn = 2.0 * np.pi * ((k1 * n2) % BLK) / BLK
    twist = np.stack([np.cos(turn), np.sin(turn)]).astype(np.float32)
    angle = 2.0 * np.pi * ((np.arange(N2)[:, None] * n2) % N2) / N2
    both = np.concatenate([np.cos(angle), np.sin(angle)], axis=1) / math.sqrt(BLK)
    high = both.astype(jnp.bfloat16)
    low = (both - high.astype(np.float64)).astype(jnp.bfloat16)
    return jnp.asarray(twist), jnp.asarray(np.stack([high, low]))


def add(a, b):
    return (a[0] + b[0], a[1] + b[1])


def sub(a, b):
    return (a[0] - b[0], a[1] - b[1])


def minus_i(a):
    return (a[1], -a[0])


def times(a, c, s):
    return (a[0] * c + a[1] * s, a[1] * c - a[0] * s)


def dft4(x):
    a, b = add(x[0], x[2]), sub(x[0], x[2])
    c, d = add(x[1], x[3]), minus_i(sub(x[1], x[3]))
    return [add(a, c), add(b, d), sub(a, c), sub(b, d)]


def dft8(x):
    even = dft4([x[0], x[2], x[4], x[6]])
    odd = dft4([x[1], x[3], x[5], x[7]])
    h = math.sqrt(0.5)
    o1, o3 = odd[1], odd[3]
    odd = [
        odd[0],
        ((o1[0] + o1[1]) * h, (o1[1] - o1[0]) * h),
        minus_i(odd[2]),
        ((o3[1] - o3[0]) * h, (-o3[0] - o3[1]) * h),
    ]
    return [add(even[k], odd[k]) for k in range(4)] + [sub(even[k], odd[k]) for k in range(4)]


def first_stage(src, lane0, row0, taps_ref, twist_ref, mid, high, low, out_row):
    rows = pl.ds(row0, 16)
    for j in range(4):
        points = []
        for a in range(8):
            n1 = 4 * a + j
            total = [None, None]
            for p in range(4):
                tap = taps_ref[pl.ds(p, 1), pl.ds(n1 * N2, N2)]
                for part in range(2):
                    at = pl.multiple_of(lane0 + p * BLK + n1 * N2, N2)
                    term = tap * src[part, rows, pl.ds(at, N2)].astype(jnp.float32)
                    total[part] = term if p == 0 else total[part] + term
            points.append(tuple(total))
        for k, value in enumerate(dft8(points)):
            if j and k:
                turn = 2.0 * math.pi * j * k / N1
                value = times(value, math.cos(turn), math.sin(turn))
            mid[0, k, j] = value[0]
            mid[1, k, j] = value[1]
    for k in range(8):
        column = dft4([(mid[0, k, j], mid[1, k, j]) for j in range(4)])
        for l, value in enumerate(column):
            k1 = k + 8 * l
            if k1:
                value = times(value, twist_ref[0, pl.ds(k1, 1), :], twist_ref[1, pl.ds(k1, 1), :])
            for dst, (re, im) in zip((high, low), split(value)):
                dst[k1, pl.ds(out_row, 16), pl.ds(0, N2)] = re
                dst[k1, pl.ds(out_row, 16), pl.ds(N2, N2)] = im
                dst[k1, pl.ds(64 + out_row, 16), pl.ds(0, N2)] = im
                dst[k1, pl.ds(64 + out_row, 16), pl.ds(N2, N2)] = -re


def split(value):
    high = tuple(v.astype(jnp.bfloat16) for v in value)
    low = tuple((v - h.astype(jnp.float32)).astype(jnp.bfloat16) for v, h in zip(value, high))
    return high, low


def second_stage(k1, dft_ref, high, low, lines):
    part = lax.dot_general(dft_ref[0], high[k1], NT, preferred_element_type=jnp.float32)
    part += lax.dot_general(dft_ref[1], high[k1], NT, preferred_element_type=jnp.float32)
    part += lax.dot_general(dft_ref[0], low[k1], NT, preferred_element_type=jnp.float32)
    lines[pl.ds(k1, N2, stride=N1), :] = part


def block_turn(picked):
    turned = picked.astype(jnp.bfloat16).T
    lane = lax.broadcasted_iota(jnp.int32, (32, 128), 1)
    low5 = (lane & 32) == 0
    low6 = (lane & 64) == 0
    c = [turned[32 * n : 32 * n + 32] for n in range(4)]

    def swap(x, y, low_lanes, step):
        return (
            jnp.where(low_lanes, x, pltpu.roll(y, step, 1)),
            jnp.where(low_lanes, pltpu.roll(x, 128 - step, 1), y),
        )

    c[0], c[1] = swap(c[0], c[1], low5, 32)
    c[2], c[3] = swap(c[2], c[3], low5, 32)
    c[0], c[2] = swap(c[0], c[2], low6, 64)
    c[1], c[3] = swap(c[1], c[3], low6, 64)
    return c


def side_work(my_bin, chan_ref, flags_ref, index_ref, table_ref, mask_ref, weight_ref, inverse_ref, twice):
    lane = lax.broadcasted_iota(jnp.int32, (8, 128), 1) & 31
    mine = jnp.zeros((8, 128), jnp.int32)
    for q in range(32):
        mine = jnp.where(lane == q, chan_ref[my_bin * 32 + q], mine)
    mine = jnp.broadcast_to(mine[0:1], (128, 128)).T
    mine = jnp.concatenate([mine] * (flags_ref.shape[1] // 128), axis=1)
    flagged = flags_ref[0:1, :] == mine
    for n in range(1, flags_ref.shape[0]):
        flagged = flagged | (flags_ref[n : n + 1, :] == mine)
    clean = jnp.where(flagged, 0.0, 1.0).T
    twice[pl.ds(0, 512, stride=2), :] = clean
    twice[pl.ds(1, 512, stride=2), :] = clean
    mask_ref[...] = twice[...].astype(jnp.bfloat16)

    @pl.loop(0, 8)
    def _(n):
        rows = pl.ds(pl.multiple_of(n * 128, 128), 128)
        counts = 2.0 * lax.dot_general(mask_ref[rows, :], mask_ref[...], NT, preferred_element_type=jnp.float32)
        inverse_ref[rows, :] = 1.0 / counts

    scale = 1.0 / math.sqrt(index_ref.shape[1])
    table = jnp.concatenate([table_ref[...], table_ref[...]], axis=1) * scale
    table_re = jnp.broadcast_to(table[0:1, :], (8, 128))
    table_im = jnp.broadcast_to(table[1:2, :], (8, 128))

    @pl.loop(0, index_ref.shape[0] // 16)
    def _(step):
        at = pl.multiple_of(step * 16, 16)
        for n in range(index_ref.shape[1] // 128):
            cols = pl.ds(n * 128, 128)
            re, im = [], []
            for half in range(2):
                index = index_ref[pl.ds(at + 8 * half, 8), cols]
                re.append(jnp.take_along_axis(table_re, index, axis=1, mode="promise_in_bounds"))
                im.append(jnp.take_along_axis(table_im, index, axis=1, mode="promise_in_bounds"))
            weight_ref[pl.ds(at, 16), cols] = jnp.concatenate(re, axis=0).astype(jnp.bfloat16)
            weight_ref[pl.ds(256 + at, 16), cols] = jnp.concatenate(im, axis=0).astype(jnp.bfloat16)


def spectra_kernel(
    chan_ref, own, history, taps_hbm, twist_hbm, dft_hbm, flags_hbm, index_hbm, table_hbm,
    vis_ref, power_ref,
    src, mid, high, low, lines, picked, out, taps_ref, twist_ref, dft_ref, flags_ref, index_ref, table_ref,
    twice, mask_ref, weight_ref, inverse_ref, arrived, lefts, rights, partial, beam_sum,
    load_sem, own_sem, rim_sem, halo_send, halo_recv, send_sem, recv_sem,
):
    grp, dev = lax.axis_index("grp"), lax.axis_index("dev")
    n_grp, n_dev = lax.axis_size("grp"), lax.axis_size("dev")
    count = n_grp * n_dev
    me = grp * n_dev + dev
    planes = [lax.rem(grp + n, n_grp) for n in range(n_grp)]
    left, right = planes[n_grp - 1], planes[1]
    is_first, is_last = grp == 0, grp == n_grp - 1
    barrier = pltpu.get_barrier_semaphore()

    for n in (1, 3, 2, 0):

        @pl.loop(0, n_dev, unroll=8)
        def _(peer):
            def greet():
                pl.semaphore_signal(
                    barrier, inc=1, device_id=(planes[n], peer), device_id_type=pl.DeviceIdType.MESH
                )

            if n:
                greet()
            else:
                pl.when(peer != dev)(greet)

    def blocks(ref, start, number, rows=slice(None)):
        return ref.at[:, rows, pl.ds(pl.multiple_of(start * BLK, BLK), number * BLK)]

    low_rows, high_rows = pl.ds(0, 16), pl.ds(16, 16)
    loads = [
        pltpu.make_async_copy(own, blocks(src, 2, 4), own_sem),
        pltpu.make_async_copy(taps_hbm, taps_ref, load_sem.at[0]),
        pltpu.make_async_copy(twist_hbm, twist_ref, load_sem.at[1]),
        pltpu.make_async_copy(dft_hbm, dft_ref, load_sem.at[2]),
        pltpu.make_async_copy(flags_hbm, flags_ref, load_sem.at[3]),
        pltpu.make_async_copy(index_hbm, index_ref, load_sem.at[4]),
        pltpu.make_async_copy(table_hbm, table_ref, load_sem.at[5]),
    ]
    for load in loads:
        load.start()
    rim_first = pltpu.make_async_copy(blocks(history, 1, 2), blocks(src, 0, 2), rim_sem)
    rim_last = pltpu.make_async_copy(blocks(history, 0, 3), blocks(src, 8, 3), rim_sem)

    @pl.when(is_first)
    def _():
        rim_first.start()

    @pl.when(is_last)
    def _():
        rim_last.start()

    def halo(block, at, rows, slot, target):
        return pltpu.make_async_remote_copy(
            src_ref=blocks(own, block, 1, rows),
            dst_ref=blocks(src, at, 1, rows),
            send_sem=halo_send.at[slot],
            recv_sem=halo_recv.at[slot],
            device_id=(target, dev),
            device_id_type=pl.DeviceIdType.MESH,
        )

    from_right = jnp.where(is_first, 11, 6)
    after = halo(0, from_right, pl.ds(0, 32), 0, left)
    beyond = halo(1, from_right + 1, high_rows, 3, left)
    near = halo(3, 1, pl.ds(0, 32), 1, right)
    far = halo(2, 0, low_rows, 2, right)

    pl.semaphore_wait(barrier, count - 1)
    after.start()

    @pl.when(jnp.logical_not(is_last))
    def _():
        near.start()

    beyond.start()

    @pl.when(jnp.logical_not(is_last))
    def _():
        far.start()

    for load in loads:
        load.wait()

    def filtered(window, line, row0):
        first_stage(src, window * BLK, row0, taps_ref, twist_ref, mid, high, low, line + row0)

    def both_halves(window, line):
        @pl.loop(0, ROWS // 16)
        def _(half):
            filtered(window, line, pl.multiple_of(half * 16, 16))

    def finish(batch):
        @pl.loop(0, N1 // 8)
        def _(step):
            for n in range(8):
                second_stage(step * 8 + n, dft_ref, high, low, lines)

        @pl.loop(0, 8)
        def _(step):
            first = lax.rem(step + dev // 4, 8) * 4
            for part in range(n_grp):
                at = planes[part] * n_dev + first
                for n in range(128):
                    picked[part, pl.ds(n, 1), :] = lines[pl.ds(chan_ref[at * 32 + n], 1), :]
                for n, block in enumerate(block_turn(picked[part])):
                    out[batch, at + n] = block.astype(jnp.bfloat16)
            for part in (2, 1, 3, 0):
                for n in range(4):
                    peer = first + n
                    place = planes[part] * n_dev + peer

                    def send():
                        pltpu.make_async_remote_copy(
                            src_ref=out.at[batch, place],
                            dst_ref=arrived.at[batch, me],
                            send_sem=send_sem.at[batch],
                            recv_sem=recv_sem.at[batch],
                            device_id=(planes[part], peer),
                            device_id_type=pl.DeviceIdType.MESH,
                        ).start()

                    if part:
                        send()
                    else:
                        pl.when(peer != dev)(send)

        pltpu.make_async_copy(out.at[batch, me], arrived.at[batch, me], recv_sem.at[batch]).start()

    both_halves(2, 0)
    side_work(me, chan_ref, flags_ref, index_ref, table_ref, mask_ref, weight_ref, inverse_ref, twice)

    @pl.when(is_last)
    def _():
        rim_last.wait()

    after.wait_recv()
    both_halves(jnp.where(is_last, 8, 3), 32)
    finish(0)

    @pl.when(is_first)
    def _():
        rim_first.wait()

    @pl.when(jnp.logical_not(is_first))
    def _():
        near.wait_recv()

    both_halves(1, 32)

    @pl.when(jnp.logical_not(is_first))
    def _():
        far.wait_recv()

    filtered(0, 0, 0)
    beyond.wait_recv()
    filtered(jnp.where(is_last, 9, 4), 0, 16)
    finish(1)

    sent = [out.at[batch, pl.ds(0, count - 1)] for batch in range(2)]
    for batch in range(2):
        pltpu.make_async_copy(arrived.at[batch], arrived.at[batch], recv_sem.at[batch]).wait()
        build(batch, arrived, mask_ref, lefts, rights)
        beam_share(batch, weight_ref, lefts, power_ref, beam_sum)

        @pl.loop(0, 4)
        def _(step):
            rows = pl.ds(pl.multiple_of(step * 256, 256), 256)
            for t in range(2):
                for part, lhs in enumerate((lefts, rights)):
                    value = lax.dot_general(lhs[t, rows, :], lefts[t], NT, preferred_element_type=jnp.float32)
                    if batch == 0:
                        partial[t, part, rows, :] = value
                    else:
                        value = (value + partial[t, part, rows, :]) * inverse_ref[rows, :]
                        vis_ref[0, t, part, rows, :] = value.astype(jnp.bfloat16)

    after.wait_send()
    beyond.wait_send()

    @pl.when(jnp.logical_not(is_last))
    def _():
        near.wait_send()
        far.wait_send()

    for batch in range(2):
        pltpu.make_async_copy(sent[batch], sent[batch], send_sem.at[batch]).wait()


def build(batch, arrived, mask_ref, lefts, rights):
    lane = lax.broadcasted_iota(jnp.int32, (256, 128), 1)
    row = lax.broadcasted_iota(jnp.int32, (256, 128), 0)
    first = (lane & 32) == 0
    moved = first & ((row & 16) != 0)

    @pl.loop(0, 4)
    def _(n):
        rows = pl.ds(pl.multiple_of(n * 256, 256), 256)
        mask = mask_ref[rows, :].astype(jnp.float32)
        held = [arrived[batch, pl.ds(g * 32 + n * 8, 8)].reshape(256, 128).astype(jnp.float32) for g in range(4)]
        if batch == 0:
            held = [held[0], jnp.where(first, held[1], held[3]), held[2], jnp.where(first, held[3], held[1])]
        else:
            held = [jnp.where(moved, held[(g + 3) % 4], held[g]) for g in range(4)]
        for g in range(4):
            masked = held[g] * mask
            crossed = pltpu.roll(masked, 64, 1)
            lanes = pl.ds(g % 2 * 128, 128)
            lefts[g // 2, rows, lanes] = masked.astype(jnp.bfloat16)
            rights[g // 2, rows, lanes] = jnp.where(lane < 64, crossed, -crossed).astype(jnp.bfloat16)


def beam_share(batch, weight_ref, lefts, power_ref, beam_sum):
    real_lane = lax.broadcasted_iota(jnp.int32, (256, 128), 1) < 64
    for t in range(2):
        product = jnp.dot(weight_ref[...], lefts[t], preferred_element_type=jnp.float32)
        total = beam_sum[t] if batch else jnp.zeros((256, 128), jnp.float32)
        for b in range(2):
            by_real = product[:256, b * 128 : b * 128 + 128]
            by_imag = pltpu.roll(product[256:, b * 128 : b * 128 + 128], 64, 1)
            beam = by_real + jnp.where(real_lane, -by_imag, by_imag)
            total += beam * beam
        if batch == 0:
            beam_sum[t] = total
        else:
            total += pltpu.roll(total, 64, 1)
            total += pltpu.roll(total, 32, 1)
            power_ref[t] = (total * 0.125).T[:32]


def spectra(chan_map, *arrays):
    anywhere = pl.BlockSpec(memory_space=pl.ANY)
    whole = pl.BlockSpec(memory_space=pltpu.VMEM)
    return pl.pallas_call(
        spectra_kernel,
        out_shape=(pltpu.VMEM((1, 2, 2, 1024, 1024), jnp.bfloat16), pltpu.VMEM((2, 32, 256), jnp.float32)),
        in_specs=[pl.BlockSpec(memory_space=pltpu.SMEM)] + [anywhere] * len(arrays),
        out_specs=(whole, whole),
        scratch_shapes=[
            pltpu.VMEM((2, ROWS, 13 * BLK), jnp.bfloat16),
            pltpu.VMEM((2, 8, 4, 16, 128), jnp.float32),
            pltpu.VMEM((N1, 128, 256), jnp.bfloat16),
            pltpu.VMEM((N1, 128, 256), jnp.bfloat16),
            pltpu.VMEM((BLK, 128), jnp.float32),
            pltpu.VMEM((4, 128, 128), jnp.float32),
            pltpu.VMEM((2, 128, 32, 128), jnp.bfloat16),
        ]
        + [pltpu.VMEM(array.shape, array.dtype) for array in arrays[2:]]
        + [
            pltpu.VMEM((1024, 128), jnp.float32),
            pltpu.VMEM((1024, 128), jnp.bfloat16),
            pltpu.VMEM((512, 1024), jnp.bfloat16),
            pltpu.VMEM((1024, 1024), jnp.float32),
            pltpu.VMEM((2, 128, 32, 128), jnp.bfloat16),
            pltpu.VMEM((2, 1024, 256), jnp.bfloat16),
            pltpu.VMEM((2, 1024, 256), jnp.bfloat16),
            pltpu.VMEM((2, 2, 1024, 1024), jnp.float32),
            pltpu.VMEM((2, 256, 128), jnp.float32),
            pltpu.SemaphoreType.DMA((6,)),
            pltpu.SemaphoreType.DMA,
            pltpu.SemaphoreType.DMA,
            pltpu.SemaphoreType.DMA((4,)),
            pltpu.SemaphoreType.DMA((4,)),
            pltpu.SemaphoreType.DMA((2,)),
            pltpu.SemaphoreType.DMA((2,)),
        ],
        compiler_params=pltpu.CompilerParams(
            vmem_limit_bytes=VMEM_LIMIT, collective_id=0, has_side_effects=True
        ),
        cost_estimate=pl.CostEstimate(flops=10**10, bytes_accessed=10**7, transcendentals=0),
        name="spectra",
    )(chan_map, *arrays)


def per_device(voltages, history, pfb_taps, chan_map, flag_lists, beam_index, beam_table):
    twist, dft = tables()
    visibilities, power = spectra(
        chan_map, voltages, history, pfb_taps, twist, dft, flag_lists.T, beam_index, beam_table
    )
    return visibilities, power.transpose(0, 2, 1)


def solution(mesh):
    placed = (P(None, "dev", "grp"), P(None, "dev", None), P(), P(), P(), P(), P())
    return jax.shard_map(
        per_device,
        mesh=mesh,
        in_specs=placed,
        out_specs=(P(("grp", "dev"), None, None, None, None), P(None, None, ("grp", "dev"))),
        check_vma=False,
    )
```

```python
import math

import numpy as np

import jax
import jax.numpy as jnp
from jax import lax
from jax.experimental import pallas as pl
from jax.experimental.pallas import tpu as pltpu
from jax.sharding import PartitionSpec as P

N1 = 32
N2 = 128
BLK = N1 * N2
ROWS = 32
FIRST_LIMIT = 32 * 1024 * 1024
LAST_LIMIT = 24 * 1024 * 1024
NT = (((1,), (1,)), ((), ()))


def tables():
    k1 = np.arange(N1)[:, None]
    n2 = np.arange(N2)[None, :]
    turn = 2.0 * np.pi * ((k1 * n2) % BLK) / BLK
    twist = np.stack([np.cos(turn), np.sin(turn)]).astype(np.float32)
    angle = 2.0 * np.pi * ((np.arange(N2)[:, None] * n2) % N2) / N2
    both = np.concatenate([np.cos(angle), np.sin(angle)], axis=1) / math.sqrt(BLK)
    high = both.astype(jnp.bfloat16)
    low = (both - high.astype(np.float64)).astype(jnp.bfloat16)
    return jnp.asarray(twist), jnp.asarray(np.stack([high, low]))


def add(a, b):
    return (a[0] + b[0], a[1] + b[1])


def sub(a, b):
    return (a[0] - b[0], a[1] - b[1])


def minus_i(a):
    return (a[1], -a[0])


def times(a, c, s):
    return (a[0] * c + a[1] * s, a[1] * c - a[0] * s)


def dft4(x):
    a, b = add(x[0], x[2]), sub(x[0], x[2])
    c, d = add(x[1], x[3]), minus_i(sub(x[1], x[3]))
    return [add(a, c), add(b, d), sub(a, c), sub(b, d)]


def dft8(x):
    even = dft4([x[0], x[2], x[4], x[6]])
    odd = dft4([x[1], x[3], x[5], x[7]])
    h = math.sqrt(0.5)
    o1, o3 = odd[1], odd[3]
    odd = [
        odd[0],
        ((o1[0] + o1[1]) * h, (o1[1] - o1[0]) * h),
        minus_i(odd[2]),
        ((o3[1] - o3[0]) * h, (-o3[0] - o3[1]) * h),
    ]
    return [add(even[k], odd[k]) for k in range(4)] + [sub(even[k], odd[k]) for k in range(4)]


def first_stage(src, lane0, row0, taps_ref, twist_ref, mid, high, low, out_row):
    rows = pl.ds(row0, 16)
    for j in range(4):
        points = []
        for a in range(8):
            n1 = 4 * a + j
            total = [None, None]
            for p in range(4):
                tap = taps_ref[pl.ds(p, 1), pl.ds(n1 * N2, N2)]
                for part in range(2):
                    at = pl.multiple_of(lane0 + p * BLK + n1 * N2, N2)
                    term = tap * src[part, rows, pl.ds(at, N2)].astype(jnp.float32)
                    total[part] = term if p == 0 else total[part] + term
            points.append(tuple(total))
        for k, value in enumerate(dft8(points)):
            if j and k:
                turn = 2.0 * math.pi * j * k / N1
                value = times(value, math.cos(turn), math.sin(turn))
            mid[0, k, j] = value[0]
            mid[1, k, j] = value[1]
    for k in range(8):
        column = dft4([(mid[0, k, j], mid[1, k, j]) for j in range(4)])
        for l, value in enumerate(column):
            k1 = k + 8 * l
            if k1:
                value = times(value, twist_ref[0, pl.ds(k1, 1), :], twist_ref[1, pl.ds(k1, 1), :])
            for dst, (re, im) in zip((high, low), split(value)):
                dst[k1, pl.ds(out_row, 16), pl.ds(0, N2)] = re
                dst[k1, pl.ds(out_row, 16), pl.ds(N2, N2)] = im
                dst[k1, pl.ds(64 + out_row, 16), pl.ds(0, N2)] = im
                dst[k1, pl.ds(64 + out_row, 16), pl.ds(N2, N2)] = -re


def split(value):
    high = tuple(v.astype(jnp.bfloat16) for v in value)
    low = tuple((v - h.astype(jnp.float32)).astype(jnp.bfloat16) for v, h in zip(value, high))
    return high, low


def second_stage(k1, dft_ref, high, low, lines):
    part = lax.dot_general(dft_ref[0], high[k1], NT, preferred_element_type=jnp.float32)
    part += lax.dot_general(dft_ref[1], high[k1], NT, preferred_element_type=jnp.float32)
    part += lax.dot_general(dft_ref[0], low[k1], NT, preferred_element_type=jnp.float32)
    lines[pl.ds(k1, N2, stride=N1), :] = part


def block_turn(picked):
    turned = picked.astype(jnp.bfloat16).T
    lane = lax.broadcasted_iota(jnp.int32, (32, 128), 1)
    low5 = (lane & 32) == 0
    low6 = (lane & 64) == 0
    c = [turned[32 * n : 32 * n + 32] for n in range(4)]

    def swap(x, y, low_lanes, step):
        return (
            jnp.where(low_lanes, x, pltpu.roll(y, step, 1)),
            jnp.where(low_lanes, pltpu.roll(x, 128 - step, 1), y),
        )

    c[0], c[1] = swap(c[0], c[1], low5, 32)
    c[2], c[3] = swap(c[2], c[3], low5, 32)
    c[0], c[2] = swap(c[0], c[2], low6, 64)
    c[1], c[3] = swap(c[1], c[3], low6, 64)
    return c


def side_work(my_bin, chan_ref, flags_ref, index_ref, table_ref, mask_ref, weight_ref, inverse_ref, twice):
    lane = lax.broadcasted_iota(jnp.int32, (8, 128), 1) & 31
    mine = jnp.zeros((8, 128), jnp.int32)
    for q in range(32):
        mine = jnp.where(lane == q, chan_ref[my_bin * 32 + q], mine)
    mine = jnp.broadcast_to(mine[0:1], (128, 128)).T
    mine = jnp.concatenate([mine] * (flags_ref.shape[1] // 128), axis=1)
    flagged = flags_ref[0:1, :] == mine
    for n in range(1, flags_ref.shape[0]):
        flagged = flagged | (flags_ref[n : n + 1, :] == mine)
    clean = jnp.where(flagged, 0.0, 1.0).T
    twice[pl.ds(0, 512, stride=2), :] = clean
    twice[pl.ds(1, 512, stride=2), :] = clean
    mask_ref[...] = twice[...].astype(jnp.bfloat16)

    @pl.loop(0, 8)
    def _(n):
        rows = pl.ds(pl.multiple_of(n * 128, 128), 128)
        counts = 2.0 * lax.dot_general(mask_ref[rows, :], mask_ref[...], NT, preferred_element_type=jnp.float32)
        inverse_ref[rows, :] = 1.0 / counts

    scale = 1.0 / math.sqrt(index_ref.shape[1])
    table = jnp.concatenate([table_ref[...], table_ref[...]], axis=1) * scale
    table_re = jnp.broadcast_to(table[0:1, :], (8, 128))
    table_im = jnp.broadcast_to(table[1:2, :], (8, 128))

    @pl.loop(0, index_ref.shape[0] // 16)
    def _(step):
        at = pl.multiple_of(step * 16, 16)
        for n in range(index_ref.shape[1] // 128):
            cols = pl.ds(n * 128, 128)
            re, im = [], []
            for half in range(2):
                index = index_ref[pl.ds(at + 8 * half, 8), cols]
                re.append(jnp.take_along_axis(table_re, index, axis=1, mode="promise_in_bounds"))
                im.append(jnp.take_along_axis(table_im, index, axis=1, mode="promise_in_bounds"))
            weight_ref[pl.ds(at, 16), cols] = jnp.concatenate(re, axis=0).astype(jnp.bfloat16)
            weight_ref[pl.ds(256 + at, 16), cols] = jnp.concatenate(im, axis=0).astype(jnp.bfloat16)


def spectra_kernel(
    chan_ref, own, history, taps_hbm, twist_hbm, dft_hbm, flags_hbm, index_hbm, table_hbm,
    lefts, rights, inverse_ref, weight_ref, beam_sum, part0, part1, part2, part3,
    src, mid, high, low, lines, picked, out, taps_ref, twist_ref, dft_ref, flags_ref, index_ref, table_ref,
    twice, mask_ref, arrived,
    load_sem, own_sem, rim_sem, halo_send, halo_recv, send_sem, recv_sem,
):
    grp, dev = lax.axis_index("grp"), lax.axis_index("dev")
    n_grp, n_dev = lax.axis_size("grp"), lax.axis_size("dev")
    count = n_grp * n_dev
    me = grp * n_dev + dev
    planes = [lax.rem(grp + n, n_grp) for n in range(n_grp)]
    left, right = planes[n_grp - 1], planes[1]
    is_first, is_last = grp == 0, grp == n_grp - 1
    barrier = pltpu.get_barrier_semaphore()

    for n in (1, 3, 2, 0):

        @pl.loop(0, n_dev, unroll=8)
        def _(peer):
            def greet():
                pl.semaphore_signal(
                    barrier, inc=1, device_id=(planes[n], peer), device_id_type=pl.DeviceIdType.MESH
                )

            if n:
                greet()
            else:
                pl.when(peer != dev)(greet)

    def blocks(ref, start, number, rows=slice(None)):
        return ref.at[:, rows, pl.ds(pl.multiple_of(start * BLK, BLK), number * BLK)]

    low_rows, high_rows = pl.ds(0, 16), pl.ds(16, 16)
    loads = [
        pltpu.make_async_copy(own, blocks(src, 2, 4), own_sem),
        pltpu.make_async_copy(taps_hbm, taps_ref, load_sem.at[0]),
        pltpu.make_async_copy(twist_hbm, twist_ref, load_sem.at[1]),
        pltpu.make_async_copy(dft_hbm, dft_ref, load_sem.at[2]),
        pltpu.make_async_copy(flags_hbm, flags_ref, load_sem.at[3]),
        pltpu.make_async_copy(index_hbm, index_ref, load_sem.at[4]),
        pltpu.make_async_copy(table_hbm, table_ref, load_sem.at[5]),
    ]
    for load in loads:
        load.start()
    rim_first = pltpu.make_async_copy(blocks(history, 1, 2), blocks(src, 0, 2), rim_sem)
    rim_last = pltpu.make_async_copy(blocks(history, 0, 3), blocks(src, 8, 3), rim_sem)

    @pl.when(is_first)
    def _():
        rim_first.start()

    @pl.when(is_last)
    def _():
        rim_last.start()

    def halo(block, at, rows, slot, target):
        return pltpu.make_async_remote_copy(
            src_ref=blocks(own, block, 1, rows),
            dst_ref=blocks(src, at, 1, rows),
            send_sem=halo_send.at[slot],
            recv_sem=halo_recv.at[slot],
            device_id=(target, dev),
            device_id_type=pl.DeviceIdType.MESH,
        )

    from_right = jnp.where(is_first, 11, 6)
    after = halo(0, from_right, pl.ds(0, 32), 0, left)
    beyond = halo(1, from_right + 1, high_rows, 3, left)
    near = halo(3, 1, pl.ds(0, 32), 1, right)
    far = halo(2, 0, low_rows, 2, right)

    pl.semaphore_wait(barrier, count - 1)
    after.start()

    @pl.when(jnp.logical_not(is_last))
    def _():
        near.start()

    beyond.start()

    @pl.when(jnp.logical_not(is_last))
    def _():
        far.start()

    for load in loads:
        load.wait()

    def filtered(window, line, row0):
        first_stage(src, window * BLK, row0, taps_ref, twist_ref, mid, high, low, line + row0)

    def both_halves(window, line):
        @pl.loop(0, ROWS // 16)
        def _(half):
            filtered(window, line, pl.multiple_of(half * 16, 16))

    def send_batch(batch):
        @pl.loop(0, N1 // 8)
        def _(step):
            for n in range(8):
                second_stage(step * 8 + n, dft_ref, high, low, lines)

        @pl.loop(0, 8)
        def _(step):
            firsts = [lax.rem(step + dev // 4 + turn, 8) * 4 for turn in (0, 3, 4, 7)]
            for part, first in enumerate(firsts):
                at = planes[part] * n_dev + first
                for n in range(128):
                    picked[part, pl.ds(n, 1), :] = lines[pl.ds(chan_ref[at * 32 + n], 1), :]
                for n, block in enumerate(block_turn(picked[part])):
                    out[batch, at + n] = block.astype(jnp.bfloat16)
            for n in range(4):
                for part in (2, 1, 3, 0):
                    peer = firsts[part] + n
                    place = planes[part] * n_dev + peer

                    def send():
                        pltpu.make_async_remote_copy(
                            src_ref=out.at[batch, place],
                            dst_ref=arrived.at[batch, me],
                            send_sem=send_sem.at[batch],
                            recv_sem=recv_sem.at[batch],
                            device_id=(planes[part], peer),
                            device_id_type=pl.DeviceIdType.MESH,
                        ).start()

                    if part:
                        send()
                    else:
                        pl.when(peer != dev)(send)

        pltpu.make_async_copy(out.at[batch, me], arrived.at[batch, me], recv_sem.at[batch]).start()

    both_halves(2, 0)
    side_work(me, chan_ref, flags_ref, index_ref, table_ref, mask_ref, weight_ref, inverse_ref, twice)

    @pl.when(is_last)
    def _():
        rim_last.wait()

    after.wait_recv()
    both_halves(jnp.where(is_last, 8, 3), 32)
    send_batch(0)

    @pl.when(is_first)
    def _():
        rim_first.wait()

    @pl.when(jnp.logical_not(is_first))
    def _():
        near.wait_recv()

    both_halves(1, 32)

    @pl.when(jnp.logical_not(is_first))
    def _():
        far.wait_recv()

    filtered(0, 0, 0)
    beyond.wait_recv()
    filtered(jnp.where(is_last, 9, 4), 0, 16)
    send_batch(1)

    pltpu.make_async_copy(arrived.at[0], arrived.at[0], recv_sem.at[0]).wait()
    build(0, arrived, mask_ref, lefts, rights)

    @pl.loop(0, 4)
    def _(step):
        rows = pl.ds(pl.multiple_of(step * 256, 256), 256)
        for t in range(2):
            for part, lhs in enumerate((lefts, rights)):
                (part0, part1, part2, part3)[2 * t + part][rows, :] = lax.dot_general(
                    lhs[t, rows, :], lefts[t], NT, preferred_element_type=jnp.float32
                )

    beam_share(weight_ref, lefts, beam_sum)
    after.wait_send()
    beyond.wait_send()

    @pl.when(jnp.logical_not(is_last))
    def _():
        near.wait_send()
        far.wait_send()

    for batch in range(2):
        sent = out.at[batch, pl.ds(0, count - 1)]
        pltpu.make_async_copy(sent, sent, send_sem.at[batch]).wait()
    pltpu.make_async_copy(arrived.at[1], arrived.at[1], recv_sem.at[1]).wait()
    build(1, arrived, mask_ref, lefts, rights)


def build(batch, arrived, mask_ref, lefts, rights):
    lane = lax.broadcasted_iota(jnp.int32, (256, 128), 1)
    row = lax.broadcasted_iota(jnp.int32, (256, 128), 0)
    first = (lane & 32) == 0
    moved = first & ((row & 16) != 0)

    @pl.loop(0, 4)
    def _(n):
        rows = pl.ds(pl.multiple_of(n * 256, 256), 256)
        mask = mask_ref[rows, :].astype(jnp.float32)
        held = [arrived[batch, pl.ds(g * 32 + n * 8, 8)].reshape(256, 128).astype(jnp.float32) for g in range(4)]
        if batch == 0:
            held = [held[0], jnp.where(first, held[1], held[3]), held[2], jnp.where(first, held[3], held[1])]
        else:
            held = [jnp.where(moved, held[(g + 3) % 4], held[g]) for g in range(4)]
        for g in range(4):
            masked = held[g] * mask
            crossed = pltpu.roll(masked, 64, 1)
            lanes = pl.ds(g % 2 * 128, 128)
            lefts[g // 2, rows, lanes] = masked.astype(jnp.bfloat16)
            rights[g // 2, rows, lanes] = jnp.where(lane < 64, crossed, -crossed).astype(jnp.bfloat16)


def beam_share(weight_ref, lefts, beam_sum, before=None):
    real_lane = lax.broadcasted_iota(jnp.int32, (256, 128), 1) < 64
    for t in range(2):
        product = jnp.dot(weight_ref[...], lefts[t], preferred_element_type=jnp.float32)
        total = jnp.zeros((256, 128), jnp.float32)
        for b in range(2):
            by_real = product[:256, b * 128 : b * 128 + 128]
            by_imag = pltpu.roll(product[256:, b * 128 : b * 128 + 128], 64, 1)
            beam = by_real + jnp.where(real_lane, -by_imag, by_imag)
            total += beam * beam
        if before is None:
            beam_sum[t] = total
        else:
            total += before[t]
            total += pltpu.roll(total, 64, 1)
            total += pltpu.roll(total, 32, 1)
            beam_sum[t] = (total * 0.125).T[:32]


def spectra(chan_map, *arrays):
    anywhere = pl.BlockSpec(memory_space=pl.ANY)
    whole = pl.BlockSpec(memory_space=pltpu.VMEM)
    return pl.pallas_call(
        spectra_kernel,
        out_shape=(
            pltpu.VMEM((2, 1024, 256), jnp.bfloat16),
            pltpu.VMEM((2, 1024, 256), jnp.bfloat16),
            pltpu.VMEM((1024, 1024), jnp.float32),
            pltpu.VMEM((512, 1024), jnp.bfloat16),
            pltpu.VMEM((2, 256, 128), jnp.float32),
        )
        + (pltpu.VMEM((1024, 1024), jnp.float32),) * 4,
        in_specs=[pl.BlockSpec(memory_space=pltpu.SMEM)] + [anywhere] * len(arrays),
        out_specs=(whole,) * 9,
        scratch_shapes=[
            pltpu.VMEM((2, ROWS, 13 * BLK), jnp.bfloat16),
            pltpu.VMEM((2, 8, 4, 16, 128), jnp.float32),
            pltpu.VMEM((N1, 128, 256), jnp.bfloat16),
            pltpu.VMEM((N1, 128, 256), jnp.bfloat16),
            pltpu.VMEM((BLK, 128), jnp.float32),
            pltpu.VMEM((4, 128, 128), jnp.float32),
            pltpu.VMEM((2, 128, 32, 128), jnp.bfloat16),
        ]
        + [pltpu.VMEM(array.shape, array.dtype) for array in arrays[2:]]
        + [
            pltpu.VMEM((1024, 128), jnp.float32),
            pltpu.VMEM((1024, 128), jnp.bfloat16),
            pltpu.VMEM((2, 128, 32, 128), jnp.bfloat16),
            pltpu.SemaphoreType.DMA((6,)),
            pltpu.SemaphoreType.DMA,
            pltpu.SemaphoreType.DMA,
            pltpu.SemaphoreType.DMA((4,)),
            pltpu.SemaphoreType.DMA((4,)),
            pltpu.SemaphoreType.DMA((2,)),
            pltpu.SemaphoreType.DMA((2,)),
        ],
        compiler_params=pltpu.CompilerParams(
            vmem_limit_bytes=FIRST_LIMIT, collective_id=0, has_side_effects=True
        ),
        cost_estimate=pl.CostEstimate(flops=10**10, bytes_accessed=10**7, transcendentals=0),
        name="spectra",
    )(chan_map, *arrays)


TILE = 128


def finish_kernel(
    lefts, rights, inverse_ref, weight_ref, before, part0, part1, part2, part3, vis_ref, power_ref, held, sems
):
    def copy(step):
        rows = pl.ds(step * TILE, TILE)
        return pltpu.make_async_copy(held.at[:, :, rows], vis_ref.at[0, :, :, rows], sems.at[step])

    for step in range(1024 // TILE):
        rows = pl.ds(step * TILE, TILE)
        for t in range(2):
            for part, lhs in enumerate((lefts, rights)):
                value = lax.dot_general(lhs[t, rows, :], lefts[t], NT, preferred_element_type=jnp.float32)
                value = (value + (part0, part1, part2, part3)[2 * t + part][rows, :]) * inverse_ref[rows, :]
                held[t, part, rows, :] = value.astype(jnp.bfloat16)
        copy(step).start()
    beam_share(weight_ref, lefts, power_ref, before)
    for step in range(1024 // TILE):
        copy(step).wait()


def finish(*arrays):
    whole = pl.BlockSpec(memory_space=pltpu.VMEM)
    return pl.pallas_call(
        finish_kernel,
        out_shape=(
            jax.ShapeDtypeStruct((1, 2, 2, 1024, 1024), jnp.bfloat16),
            jax.ShapeDtypeStruct((2, 32, 256), jnp.float32),
        ),
        in_specs=[whole] * len(arrays),
        out_specs=(pl.BlockSpec(memory_space=pl.ANY), whole),
        scratch_shapes=[
            pltpu.VMEM((2, 2, 1024, 1024), jnp.bfloat16),
            pltpu.SemaphoreType.DMA((1024 // TILE,)),
        ],
        compiler_params=pltpu.CompilerParams(vmem_limit_bytes=LAST_LIMIT),
        cost_estimate=pl.CostEstimate(flops=3 * 10**9, bytes_accessed=10**7, transcendentals=0),
        name="finish",
    )(*arrays)


def per_device(voltages, history, pfb_taps, chan_map, flag_lists, beam_index, beam_table):
    twist, dft = tables()
    shares = spectra(chan_map, voltages, history, pfb_taps, twist, dft, flag_lists.T, beam_index, beam_table)
    visibilities, power = finish(*shares)
    return visibilities, power.transpose(0, 2, 1)


def solution(mesh):
    placed = (P(None, "dev", "grp"), P(None, "dev", None), P(), P(), P(), P(), P())
    return jax.shard_map(
        per_device,
        mesh=mesh,
        in_specs=placed,
        out_specs=(P(("grp", "dev"), None, None, None, None), P(None, None, ("grp", "dev"))),
        check_vma=False,
    )
```

```python
import math

import numpy as np

import jax
import jax.numpy as jnp
from jax import lax
from jax.experimental import pallas as pl
from jax.experimental.pallas import tpu as pltpu
from jax.sharding import PartitionSpec as P

N1 = 32
N2 = 128
BLK = N1 * N2
ROWS = 32
FIRST_LIMIT = 32 * 1024 * 1024
LAST_LIMIT = 24 * 1024 * 1024
NT = (((1,), (1,)), ((), ()))


def tables():
    k1 = np.arange(N1)[:, None]
    n2 = np.arange(N2)[None, :]
    turn = 2.0 * np.pi * ((k1 * n2) % BLK) / BLK
    twist = np.stack([np.cos(turn), np.sin(turn)]).astype(np.float32)
    angle = 2.0 * np.pi * ((np.arange(N2)[:, None] * n2) % N2) / N2
    both = np.concatenate([np.cos(angle), np.sin(angle)], axis=1) / math.sqrt(BLK)
    high = both.astype(jnp.bfloat16)
    low = (both - high.astype(np.float64)).astype(jnp.bfloat16)
    return jnp.asarray(twist), jnp.asarray(np.stack([high, low]))


def add(a, b):
    return (a[0] + b[0], a[1] + b[1])


def sub(a, b):
    return (a[0] - b[0], a[1] - b[1])


def minus_i(a):
    return (a[1], -a[0])


def times(a, c, s):
    return (a[0] * c + a[1] * s, a[1] * c - a[0] * s)


def dft4(x):
    a, b = add(x[0], x[2]), sub(x[0], x[2])
    c, d = add(x[1], x[3]), minus_i(sub(x[1], x[3]))
    return [add(a, c), add(b, d), sub(a, c), sub(b, d)]


def dft8(x):
    even = dft4([x[0], x[2], x[4], x[6]])
    odd = dft4([x[1], x[3], x[5], x[7]])
    h = math.sqrt(0.5)
    o1, o3 = odd[1], odd[3]
    odd = [
        odd[0],
        ((o1[0] + o1[1]) * h, (o1[1] - o1[0]) * h),
        minus_i(odd[2]),
        ((o3[1] - o3[0]) * h, (-o3[0] - o3[1]) * h),
    ]
    return [add(even[k], odd[k]) for k in range(4)] + [sub(even[k], odd[k]) for k in range(4)]


def first_stage(src, lane0, row0, taps_ref, twist_ref, mid, high, low, out_row):
    rows = pl.ds(row0, 16)
    for j in range(4):
        points = []
        for a in range(8):
            n1 = 4 * a + j
            total = [None, None]
            for p in range(4):
                tap = taps_ref[pl.ds(p, 1), pl.ds(n1 * N2, N2)]
                for part in range(2):
                    at = pl.multiple_of(lane0 + p * BLK + n1 * N2, N2)
                    term = tap * src[part, rows, pl.ds(at, N2)].astype(jnp.float32)
                    total[part] = term if p == 0 else total[part] + term
            points.append(tuple(total))
        for k, value in enumerate(dft8(points)):
            if j and k:
                turn = 2.0 * math.pi * j * k / N1
                value = times(value, math.cos(turn), math.sin(turn))
            mid[0, k, j] = value[0]
            mid[1, k, j] = value[1]
    for k in range(8):
        column = dft4([(mid[0, k, j], mid[1, k, j]) for j in range(4)])
        for l, value in enumerate(column):
            k1 = k + 8 * l
            if k1:
                value = times(value, twist_ref[0, pl.ds(k1, 1), :], twist_ref[1, pl.ds(k1, 1), :])
            for dst, (re, im) in zip((high, low), split(value)):
                dst[k1, pl.ds(out_row, 16), pl.ds(0, N2)] = re
                dst[k1, pl.ds(out_row, 16), pl.ds(N2, N2)] = im
                dst[k1, pl.ds(64 + out_row, 16), pl.ds(0, N2)] = im
                dst[k1, pl.ds(64 + out_row, 16), pl.ds(N2, N2)] = -re


def split(value):
    high = tuple(v.astype(jnp.bfloat16) for v in value)
    low = tuple((v - h.astype(jnp.float32)).astype(jnp.bfloat16) for v, h in zip(value, high))
    return high, low


def second_stage(k1, dft_ref, high, low, lines):
    part = lax.dot_general(dft_ref[0], high[k1], NT, preferred_element_type=jnp.float32)
    part += lax.dot_general(dft_ref[1], high[k1], NT, preferred_element_type=jnp.float32)
    part += lax.dot_general(dft_ref[0], low[k1], NT, preferred_element_type=jnp.float32)
    lines[pl.ds(k1, N2, stride=N1), :] = part


def block_turn(picked):
    turned = picked.astype(jnp.bfloat16).T
    lane = lax.broadcasted_iota(jnp.int32, (32, 128), 1)
    low5 = (lane & 32) == 0
    low6 = (lane & 64) == 0
    c = [turned[32 * n : 32 * n + 32] for n in range(4)]

    def swap(x, y, low_lanes, step):
        return (
            jnp.where(low_lanes, x, pltpu.roll(y, step, 1)),
            jnp.where(low_lanes, pltpu.roll(x, 128 - step, 1), y),
        )

    c[0], c[1] = swap(c[0], c[1], low5, 32)
    c[2], c[3] = swap(c[2], c[3], low5, 32)
    c[0], c[2] = swap(c[0], c[2], low6, 64)
    c[1], c[3] = swap(c[1], c[3], low6, 64)
    return c


def side_work(my_bin, chan_ref, flags_ref, index_ref, table_ref, mask_ref, weight_ref, inverse_ref, twice):
    lane = lax.broadcasted_iota(jnp.int32, (8, 128), 1) & 31
    mine = jnp.zeros((8, 128), jnp.int32)
    for q in range(32):
        mine = jnp.where(lane == q, chan_ref[my_bin * 32 + q], mine)
    mine = jnp.broadcast_to(mine[0:1], (128, 128)).T
    mine = jnp.concatenate([mine] * (flags_ref.shape[1] // 128), axis=1)
    flagged = flags_ref[0:1, :] == mine
    for n in range(1, flags_ref.shape[0]):
        flagged = flagged | (flags_ref[n : n + 1, :] == mine)
    clean = jnp.where(flagged, 0.0, 1.0).T
    twice[pl.ds(0, 512, stride=2), :] = clean
    twice[pl.ds(1, 512, stride=2), :] = clean
    mask_ref[...] = twice[...].astype(jnp.bfloat16)

    @pl.loop(0, 8)
    def _(n):
        rows = pl.ds(pl.multiple_of(n * 128, 128), 128)
        counts = 2.0 * lax.dot_general(mask_ref[rows, :], mask_ref[...], NT, preferred_element_type=jnp.float32)
        inverse_ref[rows, :] = 1.0 / counts

    scale = 1.0 / math.sqrt(index_ref.shape[1])
    table = jnp.concatenate([table_ref[...], table_ref[...]], axis=1) * scale
    table_re = jnp.broadcast_to(table[0:1, :], (8, 128))
    table_im = jnp.broadcast_to(table[1:2, :], (8, 128))

    @pl.loop(0, index_ref.shape[0] // 16)
    def _(step):
        at = pl.multiple_of(step * 16, 16)
        for n in range(index_ref.shape[1] // 128):
            cols = pl.ds(n * 128, 128)
            re, im = [], []
            for half in range(2):
                index = index_ref[pl.ds(at + 8 * half, 8), cols]
                re.append(jnp.take_along_axis(table_re, index, axis=1, mode="promise_in_bounds"))
                im.append(jnp.take_along_axis(table_im, index, axis=1, mode="promise_in_bounds"))
            weight_ref[pl.ds(at, 16), cols] = jnp.concatenate(re, axis=0).astype(jnp.bfloat16)
            weight_ref[pl.ds(256 + at, 16), cols] = jnp.concatenate(im, axis=0).astype(jnp.bfloat16)


def spectra_kernel(
    chan_ref, own, history, taps_hbm, twist_hbm, dft_hbm, flags_hbm, index_hbm, table_hbm,
    lefts, rights, inverse_ref, weight_ref, beam_sum, part0, part1, part2, part3,
    src, mid, high, low, lines, picked, out, taps_ref, twist_ref, dft_ref, flags_ref, index_ref, table_ref,
    twice, mask_ref, arrived,
    load_sem, own_sem, rim_sem, halo_send, halo_recv, send_sem, recv_sem,
):
    grp, dev = lax.axis_index("grp"), lax.axis_index("dev")
    n_grp, n_dev = lax.axis_size("grp"), lax.axis_size("dev")
    count = n_grp * n_dev
    me = grp * n_dev + dev
    planes = [lax.rem(grp + n, n_grp) for n in range(n_grp)]
    left, right = planes[n_grp - 1], planes[1]
    is_first, is_last = grp == 0, grp == n_grp - 1
    barrier = pltpu.get_barrier_semaphore()

    for n in (1, 3, 2, 0):

        @pl.loop(0, n_dev, unroll=8)
        def _(peer):
            def greet():
                pl.semaphore_signal(
                    barrier, inc=1, device_id=(planes[n], peer), device_id_type=pl.DeviceIdType.MESH
                )

            if n:
                greet()
            else:
                pl.when(peer != dev)(greet)

    def blocks(ref, start, number, rows=slice(None)):
        return ref.at[:, rows, pl.ds(pl.multiple_of(start * BLK, BLK), number * BLK)]

    low_rows, high_rows = pl.ds(0, 16), pl.ds(16, 16)
    loads = [
        pltpu.make_async_copy(own, blocks(src, 2, 4), own_sem),
        pltpu.make_async_copy(taps_hbm, taps_ref, load_sem.at[0]),
        pltpu.make_async_copy(twist_hbm, twist_ref, load_sem.at[1]),
        pltpu.make_async_copy(dft_hbm, dft_ref, load_sem.at[2]),
        pltpu.make_async_copy(flags_hbm, flags_ref, load_sem.at[3]),
        pltpu.make_async_copy(index_hbm, index_ref, load_sem.at[4]),
        pltpu.make_async_copy(table_hbm, table_ref, load_sem.at[5]),
    ]
    for load in loads:
        load.start()
    rim_first = pltpu.make_async_copy(blocks(history, 1, 2), blocks(src, 0, 2), rim_sem)
    rim_last = pltpu.make_async_copy(blocks(history, 0, 3), blocks(src, 8, 3), rim_sem)

    @pl.when(is_first)
    def _():
        rim_first.start()

    @pl.when(is_last)
    def _():
        rim_last.start()

    def halo(block, at, rows, slot, target):
        return pltpu.make_async_remote_copy(
            src_ref=blocks(own, block, 1, rows),
            dst_ref=blocks(src, at, 1, rows),
            send_sem=halo_send.at[slot],
            recv_sem=halo_recv.at[slot],
            device_id=(target, dev),
            device_id_type=pl.DeviceIdType.MESH,
        )

    from_right = jnp.where(is_first, 11, 6)
    after = halo(0, from_right, pl.ds(0, 32), 0, left)
    beyond = halo(1, from_right + 1, high_rows, 3, left)
    near = halo(3, 1, pl.ds(0, 32), 1, right)
    far = halo(2, 0, low_rows, 2, right)

    pl.semaphore_wait(barrier, count - 1)
    after.start()

    @pl.when(jnp.logical_not(is_last))
    def _():
        near.start()

    beyond.start()

    @pl.when(jnp.logical_not(is_last))
    def _():
        far.start()

    for load in loads:
        load.wait()

    def filtered(window, line, row0):
        first_stage(src, window * BLK, row0, taps_ref, twist_ref, mid, high, low, line + row0)

    def both_halves(window, line):
        @pl.loop(0, ROWS // 16)
        def _(half):
            filtered(window, line, pl.multiple_of(half * 16, 16))

    def send_batch(batch):
        @pl.loop(0, N1 // 8)
        def _(step):
            for n in range(8):
                second_stage(step * 8 + n, dft_ref, high, low, lines)

        @pl.loop(0, 8)
        def _(step):
            firsts = [lax.rem(step + dev // 4 + turn, 8) * 4 for turn in (0, 3, 4, 7)]
            for part, first in enumerate(firsts):
                at = planes[part] * n_dev + first
                for n in range(128):
                    picked[part, pl.ds(n, 1), :] = lines[pl.ds(chan_ref[at * 32 + n], 1), :]
                for n, block in enumerate(block_turn(picked[part])):
                    out[batch, at + n] = block.astype(jnp.bfloat16)
            for n in range(4):
                for part in (2, 1, 3, 0):
                    peer = firsts[part] + n
                    place = planes[part] * n_dev + peer

                    def send():
                        pltpu.make_async_remote_copy(
                            src_ref=out.at[batch, place],
                            dst_ref=arrived.at[batch, me],
                            send_sem=send_sem.at[batch],
                            recv_sem=recv_sem.at[batch],
                            device_id=(planes[part], peer),
                            device_id_type=pl.DeviceIdType.MESH,
                        ).start()

                    if part:
                        send()
                    else:
                        pl.when(peer != dev)(send)

        pltpu.make_async_copy(out.at[batch, me], arrived.at[batch, me], recv_sem.at[batch]).start()

    both_halves(2, 0)
    side_work(me, chan_ref, flags_ref, index_ref, table_ref, mask_ref, weight_ref, inverse_ref, twice)

    @pl.when(is_last)
    def _():
        rim_last.wait()

    after.wait_recv()
    both_halves(jnp.where(is_last, 8, 3), 32)
    send_batch(0)

    @pl.when(is_first)
    def _():
        rim_first.wait()

    @pl.when(jnp.logical_not(is_first))
    def _():
        near.wait_recv()

    both_halves(1, 32)

    @pl.when(jnp.logical_not(is_first))
    def _():
        far.wait_recv()

    filtered(0, 0, 0)
    beyond.wait_recv()
    filtered(jnp.where(is_last, 9, 4), 0, 16)
    send_batch(1)

    pltpu.make_async_copy(arrived.at[0], arrived.at[0], recv_sem.at[0]).wait()
    build(0, arrived, mask_ref, lefts, rights)

    @pl.loop(0, 4)
    def _(step):
        rows = pl.ds(pl.multiple_of(step * 256, 256), 256)
        for t in range(2):
            for part, value in enumerate(products(t, rows, lefts, rights)):
                (part0, part1, part2, part3)[2 * t + part][rows, :] = value

    beam_share(weight_ref, lefts, beam_sum)
    after.wait_send()
    beyond.wait_send()

    @pl.when(jnp.logical_not(is_last))
    def _():
        near.wait_send()
        far.wait_send()

    for batch in range(2):
        sent = out.at[batch, pl.ds(0, count - 1)]
        pltpu.make_async_copy(sent, sent, send_sem.at[batch]).wait()
    pltpu.make_async_copy(arrived.at[1], arrived.at[1], recv_sem.at[1]).wait()
    build(1, arrived, mask_ref, lefts, rights)


def build(batch, arrived, mask_ref, lefts, rights):
    lane = lax.broadcasted_iota(jnp.int32, (256, 128), 1)
    row = lax.broadcasted_iota(jnp.int32, (256, 128), 0)
    first = (lane & 32) == 0
    moved = first & ((row & 16) != 0)

    @pl.loop(0, 4)
    def _(n):
        rows = pl.ds(pl.multiple_of(n * 256, 256), 256)
        mask = mask_ref[rows, :].astype(jnp.float32)
        held = [arrived[batch, pl.ds(g * 32 + n * 8, 8)].reshape(256, 128).astype(jnp.float32) for g in range(4)]
        if batch == 0:
            held = [held[0], jnp.where(first, held[1], held[3]), held[2], jnp.where(first, held[3], held[1])]
        else:
            held = [jnp.where(moved, held[(g + 3) % 4], held[g]) for g in range(4)]
        for g in range(4):
            masked = held[g] * mask
            crossed = pltpu.roll(masked, 64, 1)
            lanes = pl.ds(g % 2 * 128, 128)
            lefts[g // 2, rows, lanes] = masked.astype(jnp.bfloat16)
            rights[g // 2, rows, lanes] = jnp.where(lane < 64, crossed, -crossed).astype(jnp.bfloat16)


def products(t, rows, lefts, rights):
    both = jnp.concatenate([lefts[t, rows, :], rights[t, rows, :]], axis=0)
    value = lax.dot_general(both, lefts[t], NT, preferred_element_type=jnp.float32)
    return value[: rows.size], value[rows.size :]


def beam_share(weight_ref, lefts, beam_sum, before=None):
    real_lane = lax.broadcasted_iota(jnp.int32, (256, 128), 1) < 64
    for t in range(2):
        product = jnp.dot(weight_ref[...], lefts[t], preferred_element_type=jnp.float32)
        total = jnp.zeros((256, 128), jnp.float32)
        for b in range(2):
            by_real = product[:256, b * 128 : b * 128 + 128]
            by_imag = pltpu.roll(product[256:, b * 128 : b * 128 + 128], 64, 1)
            beam = by_real + jnp.where(real_lane, -by_imag, by_imag)
            total += beam * beam
        if before is None:
            beam_sum[t] = total
        else:
            total += before[t]
            total += pltpu.roll(total, 64, 1)
            total += pltpu.roll(total, 32, 1)
            beam_sum[t] = (total * 0.125).T[:32]


def spectra(chan_map, *arrays):
    anywhere = pl.BlockSpec(memory_space=pl.ANY)
    whole = pl.BlockSpec(memory_space=pltpu.VMEM)
    return pl.pallas_call(
        spectra_kernel,
        out_shape=(
            pltpu.VMEM((2, 1024, 256), jnp.bfloat16),
            pltpu.VMEM((2, 1024, 256), jnp.bfloat16),
            pltpu.VMEM((1024, 1024), jnp.float32),
            pltpu.VMEM((512, 1024), jnp.bfloat16),
            pltpu.VMEM((2, 256, 128), jnp.float32),
        )
        + (pltpu.VMEM((1024, 1024), jnp.float32),) * 4,
        in_specs=[pl.BlockSpec(memory_space=pltpu.SMEM)] + [anywhere] * len(arrays),
        out_specs=(whole,) * 9,
        scratch_shapes=[
            pltpu.VMEM((2, ROWS, 13 * BLK), jnp.bfloat16),
            pltpu.VMEM((2, 8, 4, 16, 128), jnp.float32),
            pltpu.VMEM((N1, 128, 256), jnp.bfloat16),
            pltpu.VMEM((N1, 128, 256), jnp.bfloat16),
            pltpu.VMEM((BLK, 128), jnp.float32),
            pltpu.VMEM((4, 128, 128), jnp.float32),
            pltpu.VMEM((2, 128, 32, 128), jnp.bfloat16),
        ]
        + [pltpu.VMEM(array.shape, array.dtype) for array in arrays[2:]]
        + [
            pltpu.VMEM((1024, 128), jnp.float32),
            pltpu.VMEM((1024, 128), jnp.bfloat16),
            pltpu.VMEM((2, 128, 32, 128), jnp.bfloat16),
            pltpu.SemaphoreType.DMA((6,)),
            pltpu.SemaphoreType.DMA,
            pltpu.SemaphoreType.DMA,
            pltpu.SemaphoreType.DMA((4,)),
            pltpu.SemaphoreType.DMA((4,)),
            pltpu.SemaphoreType.DMA((2,)),
            pltpu.SemaphoreType.DMA((2,)),
        ],
        compiler_params=pltpu.CompilerParams(
            vmem_limit_bytes=FIRST_LIMIT, collective_id=0, has_side_effects=True
        ),
        cost_estimate=pl.CostEstimate(flops=10**10, bytes_accessed=10**7, transcendentals=0),
        name="spectra",
    )(chan_map, *arrays)


TILE = 128


def finish_kernel(
    lefts, rights, inverse_ref, weight_ref, before, part0, part1, part2, part3, vis_ref, power_ref, held, sems
):
    def copy(step):
        rows = pl.ds(step * TILE, TILE)
        return pltpu.make_async_copy(held.at[:, :, rows], vis_ref.at[0, :, :, rows], sems.at[step])

    for step in range(1024 // TILE):
        rows = pl.ds(step * TILE, TILE)
        for t in range(2):
            values = products(t, rows, lefts, rights)
            for part, value in enumerate(values):
                value = (value + (part0, part1, part2, part3)[2 * t + part][rows, :]) * inverse_ref[rows, :]
                held[t, part, rows, :] = value.astype(jnp.bfloat16)
        copy(step).start()
    beam_share(weight_ref, lefts, power_ref, before)
    for step in range(1024 // TILE):
        copy(step).wait()


def finish(*arrays):
    whole = pl.BlockSpec(memory_space=pltpu.VMEM)
    return pl.pallas_call(
        finish_kernel,
        out_shape=(
            jax.ShapeDtypeStruct((1, 2, 2, 1024, 1024), jnp.bfloat16),
            jax.ShapeDtypeStruct((2, 32, 256), jnp.float32),
        ),
        in_specs=[whole] * len(arrays),
        out_specs=(pl.BlockSpec(memory_space=pl.ANY), whole),
        scratch_shapes=[
            pltpu.VMEM((2, 2, 1024, 1024), jnp.bfloat16),
            pltpu.SemaphoreType.DMA((1024 // TILE,)),
        ],
        compiler_params=pltpu.CompilerParams(vmem_limit_bytes=LAST_LIMIT),
        cost_estimate=pl.CostEstimate(flops=3 * 10**9, bytes_accessed=10**7, transcendentals=0),
        name="finish",
    )(*arrays)


def per_device(voltages, history, pfb_taps, chan_map, flag_lists, beam_index, beam_table):
    twist, dft = tables()
    shares = spectra(chan_map, voltages, history, pfb_taps, twist, dft, flag_lists.T, beam_index, beam_table)
    visibilities, power = finish(*shares)
    return visibilities, power.transpose(0, 2, 1)


def solution(mesh):
    placed = (P(None, "dev", "grp"), P(None, "dev", None), P(), P(), P(), P(), P())
    return jax.shard_map(
        per_device,
        mesh=mesh,
        in_specs=placed,
        out_specs=(P(("grp", "dev"), None, None, None, None), P(None, None, ("grp", "dev"))),
        check_vma=False,
    )
```

```python
import functools
import math

import numpy as np

import jax
import jax.numpy as jnp
from jax import lax
from jax.experimental import pallas as pl
from jax.experimental.pallas import tpu as pltpu
from jax.sharding import PartitionSpec as P

N1 = 32
N2 = 128
BLK = N1 * N2
ROWS = 32
FIRST_LIMIT = 32 * 1024 * 1024
LAST_LIMIT = 24 * 1024 * 1024
NT = (((1,), (1,)), ((), ()))


def tables():
    k1 = np.arange(N1)[:, None]
    n2 = np.arange(N2)[None, :]
    turn = 2.0 * np.pi * ((k1 * n2) % BLK) / BLK
    twist = np.stack([np.cos(turn), np.sin(turn)]).astype(np.float32)
    angle = 2.0 * np.pi * ((np.arange(N2)[:, None] * n2) % N2) / N2
    both = np.concatenate([np.cos(angle), np.sin(angle)], axis=1) / math.sqrt(BLK)
    high = both.astype(jnp.bfloat16)
    low = (both - high.astype(np.float64)).astype(jnp.bfloat16)
    return jnp.asarray(twist), jnp.asarray(np.stack([high, low]))


def add(a, b):
    return (a[0] + b[0], a[1] + b[1])


def sub(a, b):
    return (a[0] - b[0], a[1] - b[1])


def minus_i(a):
    return (a[1], -a[0])


def times(a, c, s):
    return (a[0] * c + a[1] * s, a[1] * c - a[0] * s)


def dft4(x):
    a, b = add(x[0], x[2]), sub(x[0], x[2])
    c, d = add(x[1], x[3]), minus_i(sub(x[1], x[3]))
    return [add(a, c), add(b, d), sub(a, c), sub(b, d)]


def dft8(x):
    even = dft4([x[0], x[2], x[4], x[6]])
    odd = dft4([x[1], x[3], x[5], x[7]])
    h = math.sqrt(0.5)
    o1, o3 = odd[1], odd[3]
    odd = [
        odd[0],
        ((o1[0] + o1[1]) * h, (o1[1] - o1[0]) * h),
        minus_i(odd[2]),
        ((o3[1] - o3[0]) * h, (-o3[0] - o3[1]) * h),
    ]
    return [add(even[k], odd[k]) for k in range(4)] + [sub(even[k], odd[k]) for k in range(4)]


def first_stage(src, lane0, row0, taps_ref, twist_ref, mid, high, low, out_row):
    rows = pl.ds(row0, 16)
    for j in range(4):
        points = []
        for a in range(8):
            n1 = 4 * a + j
            total = [None, None]
            for p in range(4):
                tap = taps_ref[pl.ds(p, 1), pl.ds(n1 * N2, N2)]
                for part in range(2):
                    at = pl.multiple_of(lane0 + p * BLK + n1 * N2, N2)
                    term = tap * src[part, rows, pl.ds(at, N2)].astype(jnp.float32)
                    total[part] = term if p == 0 else total[part] + term
            points.append(tuple(total))
        for k, value in enumerate(dft8(points)):
            if j and k:
                turn = 2.0 * math.pi * j * k / N1
                value = times(value, math.cos(turn), math.sin(turn))
            mid[0, k, j] = value[0]
            mid[1, k, j] = value[1]
    for k in range(8):
        column = dft4([(mid[0, k, j], mid[1, k, j]) for j in range(4)])
        for l, value in enumerate(column):
            k1 = k + 8 * l
            if k1:
                value = times(value, twist_ref[0, pl.ds(k1, 1), :], twist_ref[1, pl.ds(k1, 1), :])
            for dst, (re, im) in zip((high, low), split(value)):
                dst[k1, pl.ds(out_row, 16), pl.ds(0, N2)] = re
                dst[k1, pl.ds(out_row, 16), pl.ds(N2, N2)] = im
                dst[k1, pl.ds(64 + out_row, 16), pl.ds(0, N2)] = im
                dst[k1, pl.ds(64 + out_row, 16), pl.ds(N2, N2)] = -re


def split(value):
    high = tuple(v.astype(jnp.bfloat16) for v in value)
    low = tuple((v - h.astype(jnp.float32)).astype(jnp.bfloat16) for v, h in zip(value, high))
    return high, low


def second_stage(k1, dft_ref, high, low, lines):
    part = lax.dot_general(dft_ref[0], high[k1], NT, preferred_element_type=jnp.float32)
    part += lax.dot_general(dft_ref[1], high[k1], NT, preferred_element_type=jnp.float32)
    part += lax.dot_general(dft_ref[0], low[k1], NT, preferred_element_type=jnp.float32)
    lines[pl.ds(k1, N2, stride=N1), :] = part


def block_turn(picked):
    turned = picked.astype(jnp.bfloat16).T
    lane = lax.broadcasted_iota(jnp.int32, (32, 128), 1)
    low5 = (lane & 32) == 0
    low6 = (lane & 64) == 0
    c = [turned[32 * n : 32 * n + 32] for n in range(4)]

    def swap(x, y, low_lanes, step):
        return (
            jnp.where(low_lanes, x, pltpu.roll(y, step, 1)),
            jnp.where(low_lanes, pltpu.roll(x, 128 - step, 1), y),
        )

    c[0], c[1] = swap(c[0], c[1], low5, 32)
    c[2], c[3] = swap(c[2], c[3], low5, 32)
    c[0], c[2] = swap(c[0], c[2], low6, 64)
    c[1], c[3] = swap(c[1], c[3], low6, 64)
    return c


def side_work(my_bin, chan_ref, flags_ref, index_ref, table_ref, mask_ref, weight_ref, inverse_ref, twice):
    lane = lax.broadcasted_iota(jnp.int32, (8, 128), 1) & 31
    mine = jnp.zeros((8, 128), jnp.int32)
    for q in range(32):
        mine = jnp.where(lane == q, chan_ref[my_bin * 32 + q], mine)
    mine = jnp.broadcast_to(mine[0:1], (128, 128)).T
    mine = jnp.concatenate([mine] * (flags_ref.shape[1] // 128), axis=1)
    flagged = flags_ref[0:1, :] == mine
    for n in range(1, flags_ref.shape[0]):
        flagged = flagged | (flags_ref[n : n + 1, :] == mine)
    clean = jnp.where(flagged, 0.0, 1.0).T
    twice[pl.ds(0, 512, stride=2), :] = clean
    twice[pl.ds(1, 512, stride=2), :] = clean
    mask_ref[...] = twice[...].astype(jnp.bfloat16)

    @pl.loop(0, 8)
    def _(n):
        rows = pl.ds(pl.multiple_of(n * 128, 128), 128)
        counts = 2.0 * lax.dot_general(mask_ref[rows, :], mask_ref[...], NT, preferred_element_type=jnp.float32)
        inverse_ref[rows, :] = 1.0 / counts

    scale = 1.0 / math.sqrt(index_ref.shape[1])
    table = jnp.concatenate([table_ref[...], table_ref[...]], axis=1) * scale
    table_re = jnp.broadcast_to(table[0:1, :], (8, 128))
    table_im = jnp.broadcast_to(table[1:2, :], (8, 128))

    @pl.loop(0, index_ref.shape[0] // 16)
    def _(step):
        at = pl.multiple_of(step * 16, 16)
        for n in range(index_ref.shape[1] // 128):
            cols = pl.ds(n * 128, 128)
            re, im = [], []
            for half in range(2):
                index = index_ref[pl.ds(at + 8 * half, 8), cols]
                re.append(jnp.take_along_axis(table_re, index, axis=1, mode="promise_in_bounds"))
                im.append(jnp.take_along_axis(table_im, index, axis=1, mode="promise_in_bounds"))
            weight_ref[pl.ds(at, 16), cols] = jnp.concatenate(re, axis=0).astype(jnp.bfloat16)
            weight_ref[pl.ds(256 + at, 16), cols] = jnp.concatenate(im, axis=0).astype(jnp.bfloat16)


def spectra_kernel(
    chan_ref, own, history, taps_hbm, twist_hbm, dft_hbm, flags_hbm, index_hbm, table_hbm,
    lefts, rights, inverse_ref, weight_ref, beam_sum, part0, part1, part2, part3,
    src, mid, high, low, lines, picked, out, taps_ref, twist_ref, dft_ref, flags_ref, index_ref, table_ref,
    twice, mask_ref, arrived,
    load_sem, own_sem, rim_sem, halo_send, halo_recv, send_sem, recv_sem, entered,
):
    grp, dev = lax.axis_index("grp"), lax.axis_index("dev")
    n_grp, n_dev = lax.axis_size("grp"), lax.axis_size("dev")
    count = n_grp * n_dev
    me = grp * n_dev + dev
    planes = [lax.rem(grp + n, n_grp) for n in range(n_grp)]
    left, right = planes[n_grp - 1], planes[1]
    is_first, is_last = grp == 0, grp == n_grp - 1
    barrier = pltpu.get_barrier_semaphore()

    for n in range(1, n_grp):
        pl.semaphore_signal(barrier, inc=1, device_id=(planes[n], dev), device_id_type=pl.DeviceIdType.MESH)

    @pl.loop(0, n_dev, unroll=8)
    def _(peer):
        @pl.when(peer != dev)
        def _():
            pl.semaphore_signal(barrier, inc=1, device_id=(grp, peer), device_id_type=pl.DeviceIdType.MESH)

    def blocks(ref, start, number, rows=slice(None)):
        return ref.at[:, rows, pl.ds(pl.multiple_of(start * BLK, BLK), number * BLK)]

    low_rows, high_rows = pl.ds(0, 16), pl.ds(16, 16)
    loads = [
        pltpu.make_async_copy(own, blocks(src, 2, 4), own_sem),
        pltpu.make_async_copy(taps_hbm, taps_ref, load_sem.at[0]),
        pltpu.make_async_copy(twist_hbm, twist_ref, load_sem.at[1]),
        pltpu.make_async_copy(dft_hbm, dft_ref, load_sem.at[2]),
        pltpu.make_async_copy(flags_hbm, flags_ref, load_sem.at[3]),
        pltpu.make_async_copy(index_hbm, index_ref, load_sem.at[4]),
        pltpu.make_async_copy(table_hbm, table_ref, load_sem.at[5]),
    ]
    for load in loads:
        load.start()
    rim_first = pltpu.make_async_copy(blocks(history, 1, 2), blocks(src, 0, 2), rim_sem)
    rim_last = pltpu.make_async_copy(blocks(history, 0, 3), blocks(src, 8, 3), rim_sem)

    @pl.when(is_first)
    def _():
        rim_first.start()

    @pl.when(is_last)
    def _():
        rim_last.start()

    def halo(block, at, rows, slot, target):
        return pltpu.make_async_remote_copy(
            src_ref=blocks(own, block, 1, rows),
            dst_ref=blocks(src, at, 1, rows),
            send_sem=halo_send.at[slot],
            recv_sem=halo_recv.at[slot],
            device_id=(target, dev),
            device_id_type=pl.DeviceIdType.MESH,
        )

    from_right = jnp.where(is_first, 11, 6)
    after = halo(0, from_right, pl.ds(0, 32), 0, left)
    beyond = halo(1, from_right + 1, high_rows, 3, left)
    near = halo(3, 1, pl.ds(0, 32), 1, right)
    far = halo(2, 0, low_rows, 2, right)

    pl.semaphore_wait(barrier, n_grp + n_dev - 2)
    after.start()

    @pl.when(jnp.logical_not(is_last))
    def _():
        near.start()

    beyond.start()

    @pl.when(jnp.logical_not(is_last))
    def _():
        far.start()

    for n in range(1, n_grp):
        pl.semaphore_signal(entered, inc=1, device_id=(planes[n], dev), device_id_type=pl.DeviceIdType.MESH)

    for load in loads:
        load.wait()

    def filtered(window, line, row0):
        first_stage(src, window * BLK, row0, taps_ref, twist_ref, mid, high, low, line + row0)

    def both_halves(window, line):
        @pl.loop(0, ROWS // 16)
        def _(half):
            filtered(window, line, pl.multiple_of(half * 16, 16))

    def send_batch(batch):
        @pl.loop(0, N1 // 8)
        def _(step):
            for n in range(8):
                second_stage(step * 8 + n, dft_ref, high, low, lines)

        @pl.loop(0, 8)
        def _(step):
            firsts = [lax.rem(step + dev // 4 + turn, 8) * 4 for turn in (0, 3, 4, 7)]
            for part, first in enumerate(firsts):
                at = planes[part] * n_dev + first
                for n in range(128):
                    picked[part, pl.ds(n, 1), :] = lines[pl.ds(chan_ref[at * 32 + n], 1), :]
                for n, block in enumerate(block_turn(picked[part])):
                    out[batch, at + n] = block.astype(jnp.bfloat16)
            for n in range(4):
                for part in (2, 1, 3, 0):
                    peer = firsts[part] + n
                    place = planes[part] * n_dev + peer

                    def send():
                        pltpu.make_async_remote_copy(
                            src_ref=out.at[batch, place],
                            dst_ref=arrived.at[batch, me],
                            send_sem=send_sem.at[batch],
                            recv_sem=recv_sem.at[batch],
                            device_id=(planes[part], peer),
                            device_id_type=pl.DeviceIdType.MESH,
                        ).start()

                    if part:
                        send()
                    else:
                        pl.when(peer != dev)(send)

        pltpu.make_async_copy(out.at[batch, me], arrived.at[batch, me], recv_sem.at[batch]).start()

    both_halves(2, 0)
    side_work(me, chan_ref, flags_ref, index_ref, table_ref, mask_ref, weight_ref, inverse_ref, twice)

    @pl.when(is_last)
    def _():
        rim_last.wait()

    after.wait_recv()
    both_halves(jnp.where(is_last, 8, 3), 32)
    pl.semaphore_wait(entered, n_grp - 1)
    send_batch(0)

    @pl.when(is_first)
    def _():
        rim_first.wait()

    @pl.when(jnp.logical_not(is_first))
    def _():
        near.wait_recv()

    both_halves(1, 32)

    @pl.when(jnp.logical_not(is_first))
    def _():
        far.wait_recv()

    filtered(0, 0, 0)
    beyond.wait_recv()
    filtered(jnp.where(is_last, 9, 4), 0, 16)
    send_batch(1)

    pltpu.make_async_copy(arrived.at[0], arrived.at[0], recv_sem.at[0]).wait()
    build(0, arrived, mask_ref, lefts, rights)

    @pl.loop(0, 4)
    def _(step):
        rows = pl.ds(pl.multiple_of(step * 256, 256), 256)
        for t in range(2):
            for part, value in enumerate(products(t, rows, lefts, rights)):
                (part0, part1, part2, part3)[2 * t + part][rows, :] = value

    beam_share(weight_ref, lefts, beam_sum)
    after.wait_send()
    beyond.wait_send()

    @pl.when(jnp.logical_not(is_last))
    def _():
        near.wait_send()
        far.wait_send()

    for batch in range(2):
        sent = out.at[batch, pl.ds(0, count - 1)]
        pltpu.make_async_copy(sent, sent, send_sem.at[batch]).wait()
    pltpu.make_async_copy(arrived.at[1], arrived.at[1], recv_sem.at[1]).wait()
    build(1, arrived, mask_ref, lefts, rights)


def build(batch, arrived, mask_ref, lefts, rights):
    lane = lax.broadcasted_iota(jnp.int32, (256, 128), 1)
    row = lax.broadcasted_iota(jnp.int32, (256, 128), 0)
    first = (lane & 32) == 0
    moved = first & ((row & 16) != 0)

    @pl.loop(0, 4)
    def _(n):
        rows = pl.ds(pl.multiple_of(n * 256, 256), 256)
        mask = mask_ref[rows, :].astype(jnp.float32)
        held = [arrived[batch, pl.ds(g * 32 + n * 8, 8)].reshape(256, 128).astype(jnp.float32) for g in range(4)]
        if batch == 0:
            held = [held[0], jnp.where(first, held[1], held[3]), held[2], jnp.where(first, held[3], held[1])]
        else:
            held = [jnp.where(moved, held[(g + 3) % 4], held[g]) for g in range(4)]
        for g in range(4):
            masked = held[g] * mask
            crossed = pltpu.roll(masked, 64, 1)
            lanes = pl.ds(g % 2 * 128, 128)
            lefts[g // 2, rows, lanes] = masked.astype(jnp.bfloat16)
            rights[g // 2, rows, lanes] = jnp.where(lane < 64, crossed, -crossed).astype(jnp.bfloat16)


def products(t, rows, lefts, rights):
    both = jnp.concatenate([lefts[t, rows, :], rights[t, rows, :]], axis=0)
    value = lax.dot_general(both, lefts[t], NT, preferred_element_type=jnp.float32)
    return value[: rows.size], value[rows.size :]


def beam_share(weight_ref, lefts, beam_sum, before=None):
    real_lane = lax.broadcasted_iota(jnp.int32, (256, 128), 1) < 64
    for t in range(2):
        product = jnp.dot(weight_ref[...], lefts[t], preferred_element_type=jnp.float32)
        total = jnp.zeros((256, 128), jnp.float32)
        for b in range(2):
            by_real = product[:256, b * 128 : b * 128 + 128]
            by_imag = pltpu.roll(product[256:, b * 128 : b * 128 + 128], 64, 1)
            beam = by_real + jnp.where(real_lane, -by_imag, by_imag)
            total += beam * beam
        if before is None:
            beam_sum[t] = total
        else:
            total += before[t]
            total += pltpu.roll(total, 64, 1)
            total += pltpu.roll(total, 32, 1)
            beam_sum[t] = (total * 0.125).T[:32]


def spectra(chan_map, *arrays):
    anywhere = pl.BlockSpec(memory_space=pl.ANY)
    whole = pl.BlockSpec(memory_space=pltpu.VMEM)
    return pl.pallas_call(
        spectra_kernel,
        out_shape=(
            pltpu.VMEM((2, 1024, 256), jnp.bfloat16),
            pltpu.VMEM((2, 1024, 256), jnp.bfloat16),
            pltpu.VMEM((1024, 1024), jnp.float32),
            pltpu.VMEM((512, 1024), jnp.bfloat16),
            pltpu.VMEM((2, 256, 128), jnp.float32),
        )
        + (pltpu.VMEM((1024, 1024), jnp.float32),) * 4,
        in_specs=[pl.BlockSpec(memory_space=pltpu.SMEM)] + [anywhere] * len(arrays),
        out_specs=(whole,) * 9,
        scratch_shapes=[
            pltpu.VMEM((2, ROWS, 13 * BLK), jnp.bfloat16),
            pltpu.VMEM((2, 8, 4, 16, 128), jnp.float32),
            pltpu.VMEM((N1, 128, 256), jnp.bfloat16),
            pltpu.VMEM((N1, 128, 256), jnp.bfloat16),
            pltpu.VMEM((BLK, 128), jnp.float32),
            pltpu.VMEM((4, 128, 128), jnp.float32),
            pltpu.VMEM((2, 128, 32, 128), jnp.bfloat16),
        ]
        + [pltpu.VMEM(array.shape, array.dtype) for array in arrays[2:]]
        + [
            pltpu.VMEM((1024, 128), jnp.float32),
            pltpu.VMEM((1024, 128), jnp.bfloat16),
            pltpu.VMEM((2, 128, 32, 128), jnp.bfloat16),
            pltpu.SemaphoreType.DMA((6,)),
            pltpu.SemaphoreType.DMA,
            pltpu.SemaphoreType.DMA,
            pltpu.SemaphoreType.DMA((4,)),
            pltpu.SemaphoreType.DMA((4,)),
            pltpu.SemaphoreType.DMA((2,)),
            pltpu.SemaphoreType.DMA((2,)),
            pltpu.SemaphoreType.REGULAR,
        ],
        compiler_params=pltpu.CompilerParams(
            vmem_limit_bytes=FIRST_LIMIT, collective_id=0, has_side_effects=True
        ),
        cost_estimate=pl.CostEstimate(flops=10**10, bytes_accessed=10**7, transcendentals=0),
        name="spectra",
    )(chan_map, *arrays)


TILE = 128


def finish_kernel(
    lefts, rights, inverse_ref, weight_ref, before, part0, part1, part2, part3, vis_ref, power_ref, held, sems
):
    def copy(step):
        rows = pl.ds(step * TILE, TILE)
        return pltpu.make_async_copy(held.at[:, :, rows], vis_ref.at[0, :, :, rows], sems.at[step])

    for step in range(1024 // TILE):
        rows = pl.ds(step * TILE, TILE)
        for t in range(2):
            values = products(t, rows, lefts, rights)
            for part, value in enumerate(values):
                value = (value + (part0, part1, part2, part3)[2 * t + part][rows, :]) * inverse_ref[rows, :]
                held[t, part, rows, :] = value.astype(jnp.bfloat16)
        copy(step).start()
    beam_share(weight_ref, lefts, power_ref, before)
    for step in range(1024 // TILE):
        copy(step).wait()


def finish(*arrays):
    whole = pl.BlockSpec(memory_space=pltpu.VMEM)
    return pl.pallas_call(
        finish_kernel,
        out_shape=(
            jax.ShapeDtypeStruct((1, 2, 2, 1024, 1024), jnp.bfloat16),
            jax.ShapeDtypeStruct((2, 32, 256), jnp.float32),
        ),
        in_specs=[whole] * len(arrays),
        out_specs=(pl.BlockSpec(memory_space=pl.ANY), whole),
        scratch_shapes=[
            pltpu.VMEM((2, 2, 1024, 1024), jnp.bfloat16),
            pltpu.SemaphoreType.DMA((1024 // TILE,)),
        ],
        compiler_params=pltpu.CompilerParams(vmem_limit_bytes=LAST_LIMIT),
        cost_estimate=pl.CostEstimate(flops=3 * 10**9, bytes_accessed=10**7, transcendentals=0),
        name="finish",
    )(*arrays)


def per_device(voltages, history, pfb_taps, chan_map, flag_lists, beam_index, beam_table):
    twist, dft = tables()
    shares = spectra(chan_map, voltages, history, pfb_taps, twist, dft, flag_lists.T, beam_index, beam_table)
    visibilities, power = finish(*shares)
    return visibilities, power.transpose(0, 2, 1)


def solution(mesh):
    placed = (P(None, "dev", "grp"), P(None, "dev", None), P(), P(), P(), P(), P())
    return jax.shard_map(
        per_device,
        mesh=mesh,
        in_specs=placed,
        out_specs=(P(("grp", "dev"), None, None, None, None), P(None, None, ("grp", "dev"))),
        check_vma=False,
    )
```

```python
import math

import numpy as np

import jax
import jax.numpy as jnp
from jax import lax
from jax.experimental import pallas as pl
from jax.experimental.pallas import tpu as pltpu
from jax.sharding import PartitionSpec as P

N1 = 32
N2 = 128
BLK = N1 * N2
ROWS = 32
FIRST_LIMIT = 32 * 1024 * 1024
LAST_LIMIT = 24 * 1024 * 1024
NT = (((1,), (1,)), ((), ()))


def tables():
    k1 = np.arange(N1)[:, None]
    n2 = np.arange(N2)[None, :]
    turn = 2.0 * np.pi * ((k1 * n2) % BLK) / BLK
    twist = np.stack([np.cos(turn), np.sin(turn)]).astype(np.float32)
    angle = 2.0 * np.pi * ((np.arange(N2)[:, None] * n2) % N2) / N2
    both = np.concatenate([np.cos(angle), np.sin(angle)], axis=1) / math.sqrt(BLK)
    high = both.astype(jnp.bfloat16)
    low = (both - high.astype(np.float64)).astype(jnp.bfloat16)
    return jnp.asarray(twist), jnp.asarray(np.stack([high, low]))


def add(a, b):
    return (a[0] + b[0], a[1] + b[1])


def sub(a, b):
    return (a[0] - b[0], a[1] - b[1])


def minus_i(a):
    return (a[1], -a[0])


def times(a, c, s):
    return (a[0] * c + a[1] * s, a[1] * c - a[0] * s)


def dft4(x):
    a, b = add(x[0], x[2]), sub(x[0], x[2])
    c, d = add(x[1], x[3]), minus_i(sub(x[1], x[3]))
    return [add(a, c), add(b, d), sub(a, c), sub(b, d)]


def dft8(x):
    even = dft4([x[0], x[2], x[4], x[6]])
    odd = dft4([x[1], x[3], x[5], x[7]])
    h = math.sqrt(0.5)
    o1, o3 = odd[1], odd[3]
    odd = [
        odd[0],
        ((o1[0] + o1[1]) * h, (o1[1] - o1[0]) * h),
        minus_i(odd[2]),
        ((o3[1] - o3[0]) * h, (-o3[0] - o3[1]) * h),
    ]
    return [add(even[k], odd[k]) for k in range(4)] + [sub(even[k], odd[k]) for k in range(4)]


def first_stage(src, lane0, row0, taps_ref, twist_ref, mid, high, low, out_row):
    rows = pl.ds(row0, 16)
    for j in range(4):
        points = []
        for a in range(8):
            n1 = 4 * a + j
            total = [None, None]
            for p in range(4):
                tap = taps_ref[pl.ds(p, 1), pl.ds(n1 * N2, N2)]
                for part in range(2):
                    at = pl.multiple_of(lane0 + p * BLK + n1 * N2, N2)
                    term = tap * src[part, rows, pl.ds(at, N2)].astype(jnp.float32)
                    total[part] = term if p == 0 else total[part] + term
            points.append(tuple(total))
        for k, value in enumerate(dft8(points)):
            if j and k:
                turn = 2.0 * math.pi * j * k / N1
                value = times(value, math.cos(turn), math.sin(turn))
            mid[0, k, j] = value[0]
            mid[1, k, j] = value[1]
    for k in range(8):
        column = dft4([(mid[0, k, j], mid[1, k, j]) for j in range(4)])
        for l, value in enumerate(column):
            k1 = k + 8 * l
            if k1:
                value = times(value, twist_ref[0, pl.ds(k1, 1), :], twist_ref[1, pl.ds(k1, 1), :])
            for dst, (re, im) in zip((high, low), split(value)):
                dst[k1, pl.ds(out_row, 16), pl.ds(0, N2)] = re
                dst[k1, pl.ds(out_row, 16), pl.ds(N2, N2)] = im
                dst[k1, pl.ds(64 + out_row, 16), pl.ds(0, N2)] = im
                dst[k1, pl.ds(64 + out_row, 16), pl.ds(N2, N2)] = -re


def split(value):
    high = tuple(v.astype(jnp.bfloat16) for v in value)
    low = tuple((v - h.astype(jnp.float32)).astype(jnp.bfloat16) for v, h in zip(value, high))
    return high, low


def second_stage(k1, dft_ref, high, low, lines):
    part = lax.dot_general(dft_ref[0], high[k1], NT, preferred_element_type=jnp.float32)
    part += lax.dot_general(dft_ref[1], high[k1], NT, preferred_element_type=jnp.float32)
    part += lax.dot_general(dft_ref[0], low[k1], NT, preferred_element_type=jnp.float32)
    lines[pl.ds(k1, N2, stride=N1), :] = part


def block_turn(picked):
    turned = picked.astype(jnp.bfloat16).T
    lane = lax.broadcasted_iota(jnp.int32, (32, 128), 1)
    low5 = (lane & 32) == 0
    low6 = (lane & 64) == 0
    c = [turned[32 * n : 32 * n + 32] for n in range(4)]

    def swap(x, y, low_lanes, step):
        return (
            jnp.where(low_lanes, x, pltpu.roll(y, step, 1)),
            jnp.where(low_lanes, pltpu.roll(x, 128 - step, 1), y),
        )

    c[0], c[1] = swap(c[0], c[1], low5, 32)
    c[2], c[3] = swap(c[2], c[3], low5, 32)
    c[0], c[2] = swap(c[0], c[2], low6, 64)
    c[1], c[3] = swap(c[1], c[3], low6, 64)
    return c


def side_work(my_bin, chan_ref, flags_ref, index_ref, table_ref, mask_ref, weight_ref, inverse_ref, twice):
    lane = lax.broadcasted_iota(jnp.int32, (8, 128), 1) & 31
    mine = jnp.zeros((8, 128), jnp.int32)
    for q in range(32):
        mine = jnp.where(lane == q, chan_ref[my_bin * 32 + q], mine)
    mine = jnp.broadcast_to(mine[0:1], (128, 128)).T
    mine = jnp.concatenate([mine] * (flags_ref.shape[1] // 128), axis=1)
    flagged = flags_ref[0:1, :] == mine
    for n in range(1, flags_ref.shape[0]):
        flagged = flagged | (flags_ref[n : n + 1, :] == mine)
    clean = jnp.where(flagged, 0.0, 1.0).T
    twice[pl.ds(0, 512, stride=2), :] = clean
    twice[pl.ds(1, 512, stride=2), :] = clean
    mask_ref[...] = twice[...].astype(jnp.bfloat16)

    @pl.loop(0, 8)
    def _(n):
        rows = pl.ds(pl.multiple_of(n * 128, 128), 128)
        counts = 2.0 * lax.dot_general(mask_ref[rows, :], mask_ref[...], NT, preferred_element_type=jnp.float32)
        inverse_ref[rows, :] = 1.0 / counts

    scale = 1.0 / math.sqrt(index_ref.shape[1])
    table = jnp.concatenate([table_ref[...], table_ref[...]], axis=1) * scale
    table_re = jnp.broadcast_to(table[0:1, :], (8, 128))
    table_im = jnp.broadcast_to(table[1:2, :], (8, 128))

    @pl.loop(0, index_ref.shape[0] // 16)
    def _(step):
        at = pl.multiple_of(step * 16, 16)
        for n in range(index_ref.shape[1] // 128):
            cols = pl.ds(n * 128, 128)
            re, im = [], []
            for half in range(2):
                index = index_ref[pl.ds(at + 8 * half, 8), cols]
                re.append(jnp.take_along_axis(table_re, index, axis=1, mode="promise_in_bounds"))
                im.append(jnp.take_along_axis(table_im, index, axis=1, mode="promise_in_bounds"))
            weight_ref[pl.ds(at, 16), cols] = jnp.concatenate(re, axis=0).astype(jnp.bfloat16)
            weight_ref[pl.ds(256 + at, 16), cols] = jnp.concatenate(im, axis=0).astype(jnp.bfloat16)


def spectra_kernel(
    chan_ref, own, history, taps_hbm, twist_hbm, dft_hbm, flags_hbm, index_hbm, table_hbm,
    lefts, rights, inverse_ref, weight_ref, beam_sum, part0, part1, part2, part3,
    src, mid, high, low, lines, picked, out, taps_ref, twist_ref, dft_ref, flags_ref, index_ref, table_ref,
    twice, mask_ref, arrived,
    load_sem, own_sem, rim_sem, halo_send, halo_recv, send_sem, recv_sem, entered,
):
    grp, dev = lax.axis_index("grp"), lax.axis_index("dev")
    n_grp, n_dev = lax.axis_size("grp"), lax.axis_size("dev")
    count = n_grp * n_dev
    me = grp * n_dev + dev
    planes = [lax.rem(grp + n, n_grp) for n in range(n_grp)]
    left, right = planes[n_grp - 1], planes[1]
    is_first, is_last = grp == 0, grp == n_grp - 1
    barrier = pltpu.get_barrier_semaphore()

    for n in range(1, n_grp):
        pl.semaphore_signal(barrier, inc=1, device_id=(planes[n], dev), device_id_type=pl.DeviceIdType.MESH)

    @pl.loop(0, n_dev, unroll=8)
    def _(peer):
        @pl.when(peer != dev)
        def _():
            pl.semaphore_signal(barrier, inc=1, device_id=(grp, peer), device_id_type=pl.DeviceIdType.MESH)

    def blocks(ref, start, number, rows=slice(None)):
        return ref.at[:, rows, pl.ds(pl.multiple_of(start * BLK, BLK), number * BLK)]

    low_rows, high_rows = pl.ds(0, 16), pl.ds(16, 16)
    loads = [
        pltpu.make_async_copy(own, blocks(src, 2, 4), own_sem),
        pltpu.make_async_copy(taps_hbm, taps_ref, load_sem.at[0]),
        pltpu.make_async_copy(twist_hbm, twist_ref, load_sem.at[1]),
        pltpu.make_async_copy(dft_hbm, dft_ref, load_sem.at[2]),
        pltpu.make_async_copy(flags_hbm, flags_ref, load_sem.at[3]),
        pltpu.make_async_copy(index_hbm, index_ref, load_sem.at[4]),
        pltpu.make_async_copy(table_hbm, table_ref, load_sem.at[5]),
    ]
    for load in loads:
        load.start()
    rim_first = pltpu.make_async_copy(blocks(history, 1, 2), blocks(src, 0, 2), rim_sem)
    rim_last = pltpu.make_async_copy(blocks(history, 0, 3), blocks(src, 8, 3), rim_sem)

    @pl.when(is_first)
    def _():
        rim_first.start()

    @pl.when(is_last)
    def _():
        rim_last.start()

    def halo(block, at, rows, slot, target):
        return pltpu.make_async_remote_copy(
            src_ref=blocks(own, block, 1, rows),
            dst_ref=blocks(src, at, 1, rows),
            send_sem=halo_send.at[slot],
            recv_sem=halo_recv.at[slot],
            device_id=(target, dev),
            device_id_type=pl.DeviceIdType.MESH,
        )

    from_right = jnp.where(is_first, 11, 6)
    after = halo(0, from_right, pl.ds(0, 32), 0, left)
    beyond = halo(1, from_right + 1, high_rows, 3, left)
    near = halo(3, 1, pl.ds(0, 32), 1, right)
    far = halo(2, 0, low_rows, 2, right)

    pl.semaphore_wait(barrier, n_grp + n_dev - 2)
    after.start()

    @pl.when(jnp.logical_not(is_last))
    def _():
        near.start()

    for n in range(1, n_grp):
        pl.semaphore_signal(entered, inc=1, device_id=(planes[n], dev), device_id_type=pl.DeviceIdType.MESH)

    for load in loads:
        load.wait()

    def filtered(window, line, row0):
        first_stage(src, window * BLK, row0, taps_ref, twist_ref, mid, high, low, line + row0)

    def both_halves(window, line):
        @pl.loop(0, ROWS // 16)
        def _(half):
            filtered(window, line, pl.multiple_of(half * 16, 16))

    def send_batch(batch):
        @pl.loop(0, N1 // 16)
        def _(step):
            for n in range(16):
                second_stage(step * 16 + n, dft_ref, high, low, lines)

        @pl.loop(0, 8)
        def _(step):
            firsts = [lax.rem(step + dev // 4 + turn, 8) * 4 for turn in (0, 3, 4, 7)]
            for part, first in enumerate(firsts):
                at = planes[part] * n_dev + first
                for n in range(128):
                    picked[part, pl.ds(n, 1), :] = lines[pl.ds(chan_ref[at * 32 + n], 1), :]
                for n, block in enumerate(block_turn(picked[part])):
                    out[batch, at + n] = block.astype(jnp.bfloat16)
            for n in range(4):
                for part in (2, 1, 3, 0):
                    peer = firsts[part] + n
                    place = planes[part] * n_dev + peer

                    def send():
                        pltpu.make_async_remote_copy(
                            src_ref=out.at[batch, place],
                            dst_ref=arrived.at[batch, me],
                            send_sem=send_sem.at[batch],
                            recv_sem=recv_sem.at[batch],
                            device_id=(planes[part], peer),
                            device_id_type=pl.DeviceIdType.MESH,
                        ).start()

                    if part:
                        send()
                    else:
                        pl.when(peer != dev)(send)

        pltpu.make_async_copy(out.at[batch, me], arrived.at[batch, me], recv_sem.at[batch]).start()

    both_halves(2, 0)
    side_work(me, chan_ref, flags_ref, index_ref, table_ref, mask_ref, weight_ref, inverse_ref, twice)

    after.wait_send()
    beyond.start()

    @pl.when(jnp.logical_not(is_last))
    def _():
        near.wait_send()
        far.start()

    @pl.when(is_last)
    def _():
        rim_last.wait()

    after.wait_recv()
    both_halves(jnp.where(is_last, 8, 3), 32)
    pl.semaphore_wait(entered, n_grp - 1)
    send_batch(0)

    @pl.when(is_first)
    def _():
        rim_first.wait()

    @pl.when(jnp.logical_not(is_first))
    def _():
        near.wait_recv()

    both_halves(1, 32)

    @pl.when(jnp.logical_not(is_first))
    def _():
        far.wait_recv()

    filtered(0, 0, 0)
    beyond.wait_recv()
    filtered(jnp.where(is_last, 9, 4), 0, 16)
    send_batch(1)

    pltpu.make_async_copy(arrived.at[0], arrived.at[0], recv_sem.at[0]).wait()
    build(0, arrived, mask_ref, lefts, rights)

    @pl.loop(0, 4)
    def _(step):
        rows = pl.ds(pl.multiple_of(step * 256, 256), 256)
        for t in range(2):
            for part, value in enumerate(products(t, rows, lefts, rights)):
                (part0, part1, part2, part3)[2 * t + part][rows, :] = value

    beam_share(weight_ref, lefts, beam_sum)
    beyond.wait_send()

    @pl.when(jnp.logical_not(is_last))
    def _():
        far.wait_send()

    for batch in range(2):
        sent = out.at[batch, pl.ds(0, count - 1)]
        pltpu.make_async_copy(sent, sent, send_sem.at[batch]).wait()
    pltpu.make_async_copy(arrived.at[1], arrived.at[1], recv_sem.at[1]).wait()
    build(1, arrived, mask_ref, lefts, rights)


def build(batch, arrived, mask_ref, lefts, rights):
    lane = lax.broadcasted_iota(jnp.int32, (256, 128), 1)
    row = lax.broadcasted_iota(jnp.int32, (256, 128), 0)
    first = (lane & 32) == 0
    moved = first & ((row & 16) != 0)

    @pl.loop(0, 4)
    def _(n):
        rows = pl.ds(pl.multiple_of(n * 256, 256), 256)
        mask = mask_ref[rows, :].astype(jnp.float32)
        held = [arrived[batch, pl.ds(g * 32 + n * 8, 8)].reshape(256, 128).astype(jnp.float32) for g in range(4)]
        if batch == 0:
            held = [held[0], jnp.where(first, held[1], held[3]), held[2], jnp.where(first, held[3], held[1])]
        else:
            held = [jnp.where(moved, held[(g + 3) % 4], held[g]) for g in range(4)]
        for g in range(4):
            masked = held[g] * mask
            crossed = pltpu.roll(masked, 64, 1)
            lanes = pl.ds(g % 2 * 128, 128)
            lefts[g // 2, rows, lanes] = masked.astype(jnp.bfloat16)
            rights[g // 2, rows, lanes] = jnp.where(lane < 64, crossed, -crossed).astype(jnp.bfloat16)


def products(t, rows, lefts, rights):
    both = jnp.concatenate([lefts[t, rows, :], rights[t, rows, :]], axis=0)
    value = lax.dot_general(both, lefts[t], NT, preferred_element_type=jnp.float32)
    return value[: rows.size], value[rows.size :]


def beam_share(weight_ref, lefts, beam_sum, before=None):
    real_lane = lax.broadcasted_iota(jnp.int32, (256, 128), 1) < 64
    for t in range(2):
        product = jnp.dot(weight_ref[...], lefts[t], preferred_element_type=jnp.float32)
        total = jnp.zeros((256, 128), jnp.float32)
        for b in range(2):
            by_real = product[:256, b * 128 : b * 128 + 128]
            by_imag = pltpu.roll(product[256:, b * 128 : b * 128 + 128], 64, 1)
            beam = by_real + jnp.where(real_lane, -by_imag, by_imag)
            total += beam * beam
        if before is None:
            beam_sum[t] = total
        else:
            total += before[t]
            total += pltpu.roll(total, 64, 1)
            total += pltpu.roll(total, 32, 1)
            beam_sum[t] = (total * 0.125).T[:32]


def spectra(chan_map, *arrays):
    anywhere = pl.BlockSpec(memory_space=pl.ANY)
    whole = pl.BlockSpec(memory_space=pltpu.VMEM)
    return pl.pallas_call(
        spectra_kernel,
        out_shape=(
            pltpu.VMEM((2, 1024, 256), jnp.bfloat16),
            pltpu.VMEM((2, 1024, 256), jnp.bfloat16),
            pltpu.VMEM((1024, 1024), jnp.float32),
            pltpu.VMEM((512, 1024), jnp.bfloat16),
            pltpu.VMEM((2, 256, 128), jnp.float32),
        )
        + (pltpu.VMEM((1024, 1024), jnp.float32),) * 4,
        in_specs=[pl.BlockSpec(memory_space=pltpu.SMEM)] + [anywhere] * len(arrays),
        out_specs=(whole,) * 9,
        scratch_shapes=[
            pltpu.VMEM((2, ROWS, 13 * BLK), jnp.bfloat16),
            pltpu.VMEM((2, 8, 4, 16, 128), jnp.float32),
            pltpu.VMEM((N1, 128, 256), jnp.bfloat16),
            pltpu.VMEM((N1, 128, 256), jnp.bfloat16),
            pltpu.VMEM((BLK, 128), jnp.float32),
            pltpu.VMEM((4, 128, 128), jnp.float32),
            pltpu.VMEM((2, 128, 32, 128), jnp.bfloat16),
        ]
        + [pltpu.VMEM(array.shape, array.dtype) for array in arrays[2:]]
        + [
            pltpu.VMEM((1024, 128), jnp.float32),
            pltpu.VMEM((1024, 128), jnp.bfloat16),
            pltpu.VMEM((2, 128, 32, 128), jnp.bfloat16),
            pltpu.SemaphoreType.DMA((6,)),
            pltpu.SemaphoreType.DMA,
            pltpu.SemaphoreType.DMA,
            pltpu.SemaphoreType.DMA((4,)),
            pltpu.SemaphoreType.DMA((4,)),
            pltpu.SemaphoreType.DMA((2,)),
            pltpu.SemaphoreType.DMA((2,)),
            pltpu.SemaphoreType.REGULAR,
        ],
        compiler_params=pltpu.CompilerParams(
            vmem_limit_bytes=FIRST_LIMIT, collective_id=0, has_side_effects=True
        ),
        cost_estimate=pl.CostEstimate(flops=10**10, bytes_accessed=10**7, transcendentals=0),
        name="spectra",
    )(chan_map, *arrays)


TILE = 128


def finish_kernel(
    lefts, rights, inverse_ref, weight_ref, before, part0, part1, part2, part3, vis_ref, power_ref, held, sems
):
    def copy(step):
        rows = pl.ds(step * TILE, TILE)
        return pltpu.make_async_copy(held.at[:, :, rows], vis_ref.at[0, :, :, rows], sems.at[step])

    for step in range(1024 // TILE):
        rows = pl.ds(step * TILE, TILE)
        for t in range(2):
            values = products(t, rows, lefts, rights)
            for part, value in enumerate(values):
                value = (value + (part0, part1, part2, part3)[2 * t + part][rows, :]) * inverse_ref[rows, :]
                held[t, part, rows, :] = value.astype(jnp.bfloat16)
        copy(step).start()
    beam_share(weight_ref, lefts, power_ref, before)
    for step in range(1024 // TILE):
        copy(step).wait()


def finish(*arrays):
    whole = pl.BlockSpec(memory_space=pltpu.VMEM)
    return pl.pallas_call(
        finish_kernel,
        out_shape=(
            jax.ShapeDtypeStruct((1, 2, 2, 1024, 1024), jnp.bfloat16),
            jax.ShapeDtypeStruct((2, 32, 256), jnp.float32),
        ),
        in_specs=[whole] * len(arrays),
        out_specs=(pl.BlockSpec(memory_space=pl.ANY), whole),
        scratch_shapes=[
            pltpu.VMEM((2, 2, 1024, 1024), jnp.bfloat16),
            pltpu.SemaphoreType.DMA((1024 // TILE,)),
        ],
        compiler_params=pltpu.CompilerParams(vmem_limit_bytes=LAST_LIMIT),
        cost_estimate=pl.CostEstimate(flops=3 * 10**9, bytes_accessed=10**7, transcendentals=0),
        name="finish",
    )(*arrays)


def per_device(voltages, history, pfb_taps, chan_map, flag_lists, beam_index, beam_table):
    twist, dft = tables()
    shares = spectra(chan_map, voltages, history, pfb_taps, twist, dft, flag_lists.T, beam_index, beam_table)
    visibilities, power = finish(*shares)
    return visibilities, power.transpose(0, 2, 1)


def solution(mesh):
    placed = (P(None, "dev", "grp"), P(None, "dev", None), P(), P(), P(), P(), P())
    return jax.shard_map(
        per_device,
        mesh=mesh,
        in_specs=placed,
        out_specs=(P(("grp", "dev"), None, None, None, None), P(None, None, ("grp", "dev"))),
        check_vma=False,
    )
```
